128 devices in a mesh: fsdp: 128 (over y, z, x, core).
Axes of the slice: x: 4, y: 4, z: 4, core: 2. Of those that a mesh axis runs over, the one named last changes fastest.
Arguments:
- tokens: bfloat16 [16384, 2048], P('fsdp'), may hold values from -6 to 6
- cotangent: bfloat16 [16384, 2048], P('fsdp'), may hold values from -6 to 6
- attn_weight: float32 [2048, 8192], P('fsdp'), as said below
- mlp_weight: float32 [2048, 16896], P('fsdp'), as said below
- small_weight: float32 [7, 2048], P(None, 'fsdp'), as said below
- attn_first: float32 [2048, 8192], P('fsdp'), as said below
- attn_second: float32 [2048, 8192], P('fsdp'), as said below
- mlp_first: float32 [2048, 16896], P('fsdp'), as said below
- mlp_second: float32 [2048, 16896], P('fsdp'), as said below
- small_first: float32 [7, 2048], P(None, 'fsdp'), as said below
- small_second: float32 [7, 2048], P(None, 'fsdp'), as said below
Outputs:
- output: bfloat16 [16384, 2048], P('fsdp')
- grad_tokens: float32 [16384, 2048], P('fsdp')
- attn_new: float32 [2048, 8192], P('fsdp')
- attn_first_new: float32 [2048, 8192], P('fsdp')
- attn_second_new: float32 [2048, 8192], P('fsdp')
- mlp_new: float32 [2048, 16896], P('fsdp')
- mlp_first_new: float32 [2048, 16896], P('fsdp')
- mlp_second_new: float32 [2048, 16896], P('fsdp')
- small_new: float32 [7, 2048], P(None, 'fsdp')
- small_first_new: float32 [7, 2048], P(None, 'fsdp')
- small_second_new: float32 [7, 2048], P(None, 'fsdp')
The draws below stay inside these ranges and needn't reach their ends.
Inputs may be any that keep to these rules, and one draw needn't show every extreme that they name: `attn_weight`: projection weights of order of one over the root of their fan-in. `mlp_weight`: projection weights of order of one over the root of their fan-in. `small_weight`: norm scales near one, biases small. `attn_first`: moments of a trainer's state. `attn_second`: positive. `mlp_first`: moments of a trainer's state. `mlp_second`: positive. `small_first`: moments of a trainer's state. `small_second`: positive.
All inputs are finite; a program needn't handle non-finite values.
Results may differ from the reference program's by a relative error of at most 0.012.
Values may be sent and summed in bfloat16 or wider, within the bound.
No kernel may reach another device: no remote copies, remote signals or barrier semaphores. Data moves between devices by JAX's collectives and lax.ppermute only.
A program may use at most 896 MiB of HBM per device.

```python
import math
import jax
import jax.numpy as jnp
from jax import lax

D = 2048
HEADS = 32
HEAD = 64
ROT = 16
FF = 5632
TOK_DEV = 128
STEP = 10
TOKENS = 16384
N_FSDP = 128


def first_moment(key, shape, grad_scale):
    return 0.11 * grad_scale * jax.random.normal(key, shape, jnp.float32)


def second_moment(key, shape, grad_scale):
    factor = jnp.exp(jax.random.uniform(key, shape, jnp.float32, 0.0, math.log(4.0)))
    return 0.053 * grad_scale * grad_scale * factor


def draw_attn_weight(key, part):
    key = jax.random.fold_in(key, 11)
    base = jax.random.normal(key, (D, 4 * D), jnp.float32) * D ** (-0.5)
    column = jnp.arange(4 * D)[None, :]
    return jnp.where(column >= 3 * D, 4.0 * base, base)


def draw_mlp_weight(key, part):
    key = jax.random.fold_in(key, 12)
    base = jax.random.normal(key, (D, 3 * FF), jnp.float32) * D ** (-0.5)
    column = jnp.arange(3 * FF)[None, :]
    return jnp.where(column >= 2 * FF, base * (D / FF) ** 0.5, base)


def draw_small_weight(key, part):
    key = jax.random.fold_in(key, 13)
    noise = jnp.clip(jax.random.normal(key, (7, D), jnp.float32), -4.0, 4.0)
    row = jnp.arange(7)[:, None]
    gains = 1.0 + 0.15 * noise
    shifts = 0.2 * noise
    biases = 0.3 * noise
    return jnp.where((row == 0) | (row == 2), gains, jnp.where((row == 1) | (row == 3), shifts, biases))


def draw_attn_first(key, part):
    key = jax.random.fold_in(key, 14)
    return first_moment(key, (D, 4 * D), math.sqrt(TOKENS))


def draw_attn_second(key, part):
    key = jax.random.fold_in(key, 15)
    return second_moment(key, (D, 4 * D), math.sqrt(TOKENS))


def draw_mlp_first(key, part):
    key = jax.random.fold_in(key, 16)
    return first_moment(key, (D, 3 * FF), 0.5 * math.sqrt(TOKENS))


def draw_mlp_second(key, part):
    key = jax.random.fold_in(key, 17)
    return second_moment(key, (D, 3 * FF), 0.5 * math.sqrt(TOKENS))


def draw_small_first(key, part):
    key = jax.random.fold_in(key, 18)
    return first_moment(key, (7, D), math.sqrt(TOKENS))


def draw_small_second(key, part):
    key = jax.random.fold_in(key, 19)
    return second_moment(key, (7, D), math.sqrt(TOKENS))


def shard_levels(own_key, dims, split, low, top_value):
    factor_of, own = 1.0, jax.random.fold_in(own_key, 6)
    for axis_at, parts in split:
        draws = jnp.exp(jax.random.uniform(jax.random.fold_in(own, axis_at), (parts,), jnp.float32, low / len(split), top_value / len(split)))
        factor_of = factor_of * jnp.repeat(draws, dims[axis_at] // parts).reshape([-1 if axis == axis_at else 1 for axis in range(len(dims))])
    return factor_of


def gaussian(stream_key, extent, deviation, most, split=(), held_as=jnp.bfloat16):
    drawn = deviation * jax.random.normal(stream_key, extent, jnp.float32)
    if split:
        drawn = drawn * shard_levels(stream_key, extent, split, -0.22, 0.18)
    return jnp.clip(drawn, -most, most).astype(held_as)


def setup_inputs(seed: int = 0) -> dict:
    splits = jax.random.split(jax.random.key(seed), 12)
    return {
        "tokens": gaussian(splits[0], (TOKENS, D), 1.0, 6.0, ((0, 128),)),
        "cotangent": gaussian(splits[1], (TOKENS, D), 1.0, 6.0, ((0, 128),)),
        "attn_weight": draw_attn_weight(jax.random.fold_in(splits[11], 71), 0),
        "mlp_weight": draw_mlp_weight(jax.random.fold_in(splits[11], 71), 0),
        "small_weight": draw_small_weight(jax.random.fold_in(splits[11], 71), 0),
        "attn_first": draw_attn_first(jax.random.fold_in(splits[11], 71), 0),
        "attn_second": draw_attn_second(jax.random.fold_in(splits[11], 71), 0),
        "mlp_first": draw_mlp_first(jax.random.fold_in(splits[11], 71), 0),
        "mlp_second": draw_mlp_second(jax.random.fold_in(splits[11], 71), 0),
        "small_first": draw_small_first(jax.random.fold_in(splits[11], 71), 0),
        "small_second": draw_small_second(jax.random.fold_in(splits[11], 71), 0),
    }


norm_eps = 1e-05
mask_fill = -1000000000.0
rope_base = 10000.0
beta_one = 0.9
beta_two = 0.95
adam_eps = 1e-08
rate_matrix = 0.01
rate_small = 0.1
decay_matrix = 0.1

@jax.custom_vjp
def low(v):
    return lax.optimization_barrier(v.astype(jnp.bfloat16)).astype(jnp.float32)

@jax.custom_vjp
def low_back(v):
    return v

def low_keep(v):
    return (low(v), None)

def low_pass(kept, grad):
    return (grad,)

def back_keep(v):
    return (v, None)

def back_low(kept, grad):
    return (low(grad),)
low.defvjp(low_keep, low_pass)
low_back.defvjp(back_keep, back_low)

def product(left, right):
    return jnp.dot(left, right, precision=lax.Precision.HIGHEST, preferred_element_type=jnp.float32)

def layer_norm(values, gain, shift):
    center = values - lax.optimization_barrier(jnp.mean(values, axis=-1, keepdims=True))
    spread = lax.optimization_barrier(jnp.mean(center * center, axis=-1, keepdims=True))
    return center * lax.rsqrt(spread + norm_eps) * gain + shift

def rope_tables(length):
    half = ROT // 2
    position = jnp.arange(length).astype(jnp.float32)
    inverse = rope_base ** (-(jnp.arange(half).astype(jnp.float32) * 2.0 / ROT))
    angle = position[:, None] * inverse[None, :]
    return (jnp.cos(angle), jnp.sin(angle))

def turn(tensor, cosine, sine, sign):
    half = ROT // 2
    first = tensor[..., :half]
    second = tensor[..., half:ROT]
    cos_b = cosine[:, None, :]
    sin_b = sine[:, None, :] * sign
    return jnp.concatenate([first * cos_b - second * sin_b, second * cos_b + first * sin_b, tensor[..., ROT:]], axis=-1)

def attend_one(pieces):
    query, keyed, valued = pieces
    length = query.shape[0]
    scores = jnp.einsum('qhe,khe->hqk', query, keyed, precision=lax.Precision.HIGHEST) * HEAD ** (-0.5)
    causal = jnp.arange(length)[:, None] >= jnp.arange(length)[None, :]
    scores = low_back(jnp.where(causal[None], scores, mask_fill))
    top = lax.optimization_barrier(jnp.max(scores, axis=-1, keepdims=True))
    weights = jnp.exp(scores - top)
    total = lax.optimization_barrier(jnp.sum(weights, axis=-1, keepdims=True))
    prob = low(weights / total)
    return jnp.einsum('hqk,khe->qhe', prob, valued, precision=lax.Precision.HIGHEST)

def forward(attn_weight, mlp_weight, small_weight, inputs):
    attn_low = low(attn_weight)
    mlp_low = low(mlp_weight)
    small_low = low(small_weight)
    normed = low(layer_norm(inputs, small_low[0], small_low[1]))
    bias = jnp.concatenate([small_low[4], small_low[5], small_low[6]])
    projected = low_back(product(normed, attn_low[:, :3 * D]) + bias)
    cosine, sine = rope_tables(TOK_DEV)
    shaped = projected.reshape(N_FSDP, TOK_DEV, 3, HEADS, HEAD)
    query = low(turn(shaped[:, :, 0], cosine, sine, 1.0))
    keyed = low(turn(shaped[:, :, 1], cosine, sine, 1.0))
    valued = low(shaped[:, :, 2])
    mixed = lax.map(jax.checkpoint(attend_one), (query, keyed, valued))
    mixed = low(low_back(mixed.reshape(TOKENS, D)))
    residual = inputs + low_back(product(mixed, attn_low[:, 3 * D:]))
    normed_two = low(layer_norm(residual, small_low[2], small_low[3]))
    gate = low_back(product(normed_two, mlp_low[:, :FF]))
    upward = low_back(product(normed_two, mlp_low[:, FF:2 * FF]))
    hidden = low(jax.nn.silu(gate) * upward)
    return residual + product(hidden, mlp_low[:, 2 * FF:].T)

def adamw(weight, grad, first, second, rate, decay):
    first_new = beta_one * first + (1.0 - beta_one) * grad
    second_new = beta_two * second + (1.0 - beta_two) * grad * grad
    corr_one = 1.0 - beta_one ** STEP
    corr_two = 1.0 - beta_two ** STEP
    update = first_new / corr_one / (jnp.sqrt(second_new / corr_two) + adam_eps)
    return (weight - rate * (update + decay * weight), first_new, second_new)

def reference(tokens, cotangent, attn_weight, mlp_weight, small_weight, attn_first, attn_second, mlp_first, mlp_second, small_first, small_second):
    output, pull = jax.vjp(forward, attn_weight, mlp_weight, small_weight, tokens.astype(jnp.float32))
    grad_attn, grad_mlp, grad_small, grad_tokens = pull(cotangent.astype(jnp.float32))
    attn_new, attn_first_new, attn_second_new = adamw(attn_weight, grad_attn, attn_first, attn_second, rate_matrix, decay_matrix)
    mlp_new, mlp_first_new, mlp_second_new = adamw(mlp_weight, grad_mlp, mlp_first, mlp_second, rate_matrix, decay_matrix)
    small_new, small_first_new, small_second_new = adamw(small_weight, grad_small, small_first, small_second, rate_small, 0.0)
    return (output.astype(jnp.bfloat16), grad_tokens, attn_new, attn_first_new, attn_second_new, mlp_new, mlp_first_new, mlp_second_new, small_new, small_first_new, small_second_new)
```

```python
import jax
import jax.numpy as jnp
from jax import lax
from jax.sharding import Mesh, PartitionSpec as P

HEAD = 64
ROT = 16
STEP = 10

norm_eps = 1e-05
mask_fill = -1000000000.0
rope_base = 10000.0
beta_one = 0.9
beta_two = 0.95
adam_eps = 1e-08
rate_matrix = 0.01
rate_small = 0.1
decay_matrix = 0.1

LOW = jnp.bfloat16
FULL = jnp.float32

OUTER = ("y", "z")
GROUP = ("x", "core")
EVERY = OUTER + GROUP
RING = 4
MEMBERS = 8
OUTERS = 16


def product(left, right, dims):
    return lax.dot_general(left, right, (dims, ((), ())), preferred_element_type=FULL)


def normalize(values):
    center = values - jnp.mean(values, axis=-1, keepdims=True)
    spread = jnp.mean(center * center, axis=-1, keepdims=True)
    scaled = lax.rsqrt(spread + norm_eps)
    return (center * scaled, scaled)


def norm_back(grad_normed, normal, scaled, gain):
    grad_hat = grad_normed * gain
    back = scaled * (
        grad_hat
        - jnp.mean(grad_hat, axis=-1, keepdims=True)
        - normal * jnp.mean(grad_hat * normal, axis=-1, keepdims=True)
    )
    return (back, jnp.sum(grad_normed * normal, axis=0), jnp.sum(grad_normed, axis=0))


def rope_tables(length):
    half = ROT // 2
    position = jnp.arange(length).astype(FULL)
    inverse = rope_base ** (-(jnp.arange(half).astype(FULL) * 2.0 / ROT))
    angle = position[:, None] * inverse[None, :]
    return (jnp.cos(angle), jnp.sin(angle))


def turn(tensor, cosine, sine, sign):
    half = ROT // 2
    first = tensor[..., :half]
    second = tensor[..., half:ROT]
    cos_b = cosine[:, None, :]
    sin_b = sine[:, None, :] * sign
    return jnp.concatenate(
        [first * cos_b - second * sin_b, second * cos_b + first * sin_b, tensor[..., ROT:]], axis=-1
    )


def attend_forward(query, keyed, valued):
    length = query.shape[1]
    factor = query.shape[-1] ** (-0.5)
    scores = jnp.einsum("sqhe,skhe->shqk", query, keyed, preferred_element_type=FULL) * factor
    causal = jnp.arange(length)[:, None] >= jnp.arange(length)[None, :]
    scores = jnp.where(causal, scores, mask_fill)
    top = jnp.max(scores, axis=-1, keepdims=True)
    weights = jnp.exp(scores - top)
    total = jnp.sum(weights, axis=-1, keepdims=True)
    prob = weights / total
    prob_low = prob.astype(LOW)
    outs = jnp.einsum("shqk,skhe->sqhe", prob_low, valued, preferred_element_type=FULL)
    return (outs, prob)


def attend_backward(query, keyed, valued, grad_mixed, prob):
    factor = query.shape[-1] ** (-0.5)
    prob_low = prob.astype(LOW)
    grad_value = jnp.einsum("shqk,sqhe->skhe", prob_low, grad_mixed, preferred_element_type=FULL)
    grad_prob = jnp.einsum("sqhe,skhe->shqk", grad_mixed, valued, preferred_element_type=FULL)
    delta = jnp.sum(prob * grad_prob, axis=-1, keepdims=True)
    grad_scores = (prob * (grad_prob - delta)).astype(LOW)
    grad_query = (
        jnp.einsum("shqk,skhe->sqhe", grad_scores, keyed, preferred_element_type=FULL) * factor
    )
    grad_key = (
        jnp.einsum("shqk,sqhe->skhe", grad_scores, query, preferred_element_type=FULL) * factor
    )
    return (grad_query, grad_key, grad_value)


def adamw(weight, grad, first, second, rate, decay):
    first_new = beta_one * first + (1.0 - beta_one) * grad
    second_new = beta_two * second + (1.0 - beta_two) * grad * grad
    corr_one = 1.0 - beta_one**STEP
    corr_two = 1.0 - beta_two**STEP
    update = first_new / corr_one / (jnp.sqrt(second_new / corr_two) + adam_eps)
    return (weight - rate * (update + decay * weight), first_new, second_new)


def ring(values, hop):
    return lax.ppermute(values, "x", [(i, (i + hop) % RING) for i in range(RING)])


def sibling(values):
    return lax.ppermute(values, "core", [(0, 1), (1, 0)])


def gather_group(values):
    half = values.shape[0] // 2
    before = ring(values, 1)
    after = ring(values, -1)
    twin = sibling(values)
    far = jnp.concatenate([ring(before[:half], 1), ring(after[half:], -1)], axis=0)
    near = jnp.concatenate([before, after], axis=0)
    near_twin = sibling(near)
    far_twin = sibling(far)
    rows = values.shape[0]
    return jnp.concatenate(
        [values, twin, before, near_twin[:rows], after, near_twin[rows:], far, far_twin], axis=0
    )


def scatter_group(parts):
    rows = parts.shape[0] // MEMBERS
    half = rows // 2
    pieces = parts.reshape(RING, 2, rows, -1)
    mine, other = (pieces[:, 0], pieces[:, 1])
    far = mine[3].astype(FULL) + sibling(other[3]).astype(FULL)
    far = far.astype(LOW)
    up = ring(far[:half], 1)
    down = ring(far[half:], -1)
    both = sibling(other[:3]).astype(FULL) + mine[:3].astype(FULL)
    zero = jnp.zeros_like(up, dtype=FULL)
    to_after = (both[2] + jnp.concatenate([up.astype(FULL), zero], axis=0)).astype(LOW)
    to_before = (both[1] + jnp.concatenate([zero, down.astype(FULL)], axis=0)).astype(LOW)
    return both[0] + ring(to_after, 1).astype(FULL) + ring(to_before, -1).astype(FULL)


def block_moves(back):
    moves = []
    for outer in range(OUTERS):
        for member in range(MEMBERS):
            owner = member * OUTERS + outer
            here = outer * MEMBERS + member
            moves.append((here, owner) if back else (owner, here))
    return moves


def spread_columns(block, parts):
    rows = block.shape[0]
    return block.reshape(rows, parts, MEMBERS, -1).transpose(2, 0, 1, 3).reshape(MEMBERS, rows, -1)


def join_columns(pieces, parts):
    members, rows, width = pieces.shape
    turned = pieces.reshape(members, rows, parts, width // parts).transpose(1, 2, 0, 3)
    return turned.reshape(rows, members * width)


def local(
    tokens,
    cotangent,
    attn_weight,
    mlp_weight,
    small_weight,
    attn_first,
    attn_second,
    mlp_first,
    mlp_second,
    small_first,
    small_second,
):
    length, width = tokens.shape
    own_rows = attn_weight.shape[0]
    slab = own_rows * MEMBERS
    hidden = mlp_weight.shape[1] // 3 // MEMBERS
    inner = width // MEMBERS
    heads = inner // HEAD
    member = lax.axis_index(GROUP)

    attn_low = attn_weight.astype(LOW)
    small_low = jnp.pad(small_weight.astype(LOW).T, ((0, 0), (0, 121)))
    sent = jnp.concatenate(
        [spread_columns(attn_low[:, : 3 * width], 3), jnp.broadcast_to(small_low, (MEMBERS, own_rows, 128))],
        axis=2,
    )
    attn_slab = lax.all_to_all(sent, GROUP, 0, 0, tiled=True).reshape(slab, 3 * inner + 128)
    out_block = lax.ppermute(attn_low[:, 3 * width :], EVERY, block_moves(False))
    out_block = out_block.reshape(own_rows, MEMBERS, inner).transpose(1, 0, 2).reshape(slab, inner)
    attn_part = lax.all_gather(
        jnp.concatenate([attn_slab, out_block], axis=1), OUTER, axis=0, tiled=True
    )
    mlp_slab = lax.all_to_all(
        spread_columns(mlp_weight.astype(LOW), 3), GROUP, 0, 0, tiled=True
    ).reshape(slab, 3 * hidden)
    mlp_part = lax.all_gather(mlp_slab, OUTER, axis=0, tiled=True)
    weight_in = attn_part[:, : 3 * inner]
    params = attn_part[:, 3 * inner : 3 * inner + 7].T.astype(FULL)
    weight_out = (
        attn_part[:, 3 * inner + 128 :]
        .reshape(OUTERS, MEMBERS, own_rows, inner)
        .transpose(0, 2, 1, 3)
        .reshape(inner, width)
    )
    bias = lax.dynamic_slice_in_dim(params[4:7], member * inner, inner, axis=1).reshape(-1)
    weight_wide = mlp_part[:, : 2 * hidden]
    weight_down = mlp_part[:, 2 * hidden :]

    tokens_all = gather_group(tokens)
    cotangent_all = gather_group(cotangent)
    normal_all, _ = normalize(tokens_all.astype(FULL))
    normed_low = (normal_all * params[0] + params[1]).astype(LOW)
    projected = product(normed_low, weight_in, ((1,), (0,))) + bias
    shaped = projected.reshape(MEMBERS, length, 3, heads, HEAD)
    cosine, sine = rope_tables(length)
    query_low = turn(shaped[:, :, 0], cosine, sine, 1.0).astype(LOW)
    key_low = turn(shaped[:, :, 1], cosine, sine, 1.0).astype(LOW)
    value_low = shaped[:, :, 2].astype(LOW)
    mixed, prob = attend_forward(query_low, key_low, value_low)
    mixed_low = mixed.reshape(-1, inner).astype(LOW)
    inputs = tokens.astype(FULL)
    residual = inputs + scatter_group(product(mixed_low, weight_out, ((1,), (0,))).astype(LOW))

    normal_two, scaled_two = normalize(residual)
    normed_two = gather_group((normal_two * params[2] + params[3]).astype(LOW))
    both = product(normed_two, weight_wide, ((1,), (0,)))
    gate, upward = (both[:, :hidden], both[:, hidden:])
    sigma = jax.nn.sigmoid(gate)
    active = gate * sigma
    hidden_low = (active * upward).astype(LOW)
    back_hidden = product(cotangent_all, weight_down, ((1,), (0,)))
    back_wide = jnp.concatenate(
        [
            (back_hidden * upward * sigma * (1.0 + gate * (1.0 - sigma))).astype(LOW),
            (back_hidden * active).astype(LOW),
        ],
        axis=1,
    )
    back_normed_two = scatter_group(product(back_wide, weight_wide, ((1,), (1,))).astype(LOW))
    output = residual + scatter_group(product(hidden_low, weight_down, ((1,), (1,))).astype(LOW))
    mlp_grad = jnp.concatenate(
        [
            product(normed_two, back_wide, ((0,), (0,))).astype(LOW),
            product(cotangent_all, hidden_low, ((0,), (0,))).astype(LOW),
        ],
        axis=1,
    )
    mlp_grad = lax.psum_scatter(mlp_grad, OUTER, scatter_dimension=0, tiled=True)
    back_residual, gain_two_grad, shift_two_grad = norm_back(
        back_normed_two, normal_two, scaled_two, params[2]
    )
    back_residual = cotangent.astype(FULL) + back_residual

    back_branch = gather_group(back_residual.astype(LOW))
    grad_out = product(mixed_low, back_branch, ((0,), (0,)))
    back_mixed = (
        product(back_branch, weight_out, ((1,), (1,)))
        .astype(LOW)
        .reshape(MEMBERS, length, heads, HEAD)
    )
    back_query, back_key, back_value = attend_backward(
        query_low, key_low, value_low, back_mixed, prob
    )
    back_query = turn(back_query, cosine, sine, -1.0)
    back_key = turn(back_key, cosine, sine, -1.0)
    back_proj = jnp.concatenate(
        [
            back_query.reshape(-1, inner),
            back_key.reshape(-1, inner),
            back_value.reshape(-1, inner),
        ],
        axis=1,
    ).astype(LOW)
    bias_grad = jnp.sum(back_proj, axis=0, dtype=FULL)
    grad_in = product(normed_low, back_proj, ((0,), (0,)))
    back_normed_one = scatter_group(product(back_proj, weight_in, ((1,), (1,))).astype(LOW))
    normal_one, scaled_one = normalize(inputs)
    back_inputs, gain_one_grad, shift_one_grad = norm_back(
        back_normed_one, normal_one, scaled_one, params[0]
    )
    grad_tokens = back_residual + back_inputs

    norm_grads = jnp.stack([gain_one_grad, shift_one_grad, gain_two_grad, shift_two_grad], axis=1)
    bias_rows = jnp.pad(
        bias_grad.reshape(3, OUTERS, own_rows).transpose(1, 2, 0),
        ((0, 0), (0, slab - own_rows), (0, 0)),
    ).reshape(width, 3)
    small_rows = jnp.pad(jnp.concatenate([norm_grads, bias_rows], axis=1), ((0, 0), (0, 121)))
    grad_out = (
        grad_out.reshape(OUTERS, own_rows, MEMBERS, inner)
        .transpose(0, 2, 1, 3)
        .reshape(width, inner)
    )
    attn_grad = jnp.concatenate(
        [grad_in.astype(LOW), small_rows.astype(LOW), grad_out.astype(LOW)], axis=1
    )
    attn_grad = lax.psum_scatter(attn_grad, OUTER, scatter_dimension=0, tiled=True)
    out_grad = (
        attn_grad[:, 3 * inner + 128 :]
        .reshape(MEMBERS, own_rows, inner)
        .transpose(1, 0, 2)
        .reshape(own_rows, width)
    )
    bias_grad = attn_grad[:own_rows, 3 * inner : 3 * inner + 128]
    block = lax.ppermute(
        jnp.concatenate([out_grad, bias_grad], axis=1), EVERY, block_moves(True)
    ).astype(FULL)
    pieces = lax.all_to_all(
        attn_grad[:, : 3 * inner + 128].reshape(MEMBERS, own_rows, -1), GROUP, 0, 0, tiled=True
    ).astype(FULL)
    attn_grad = jnp.concatenate(
        [join_columns(pieces[:, :, : 3 * inner], 3), block[:, :width]], axis=1
    )
    norm_grads = jnp.sum(pieces[:, :, 3 * inner : 3 * inner + 4], axis=0)
    small_grad = jnp.concatenate([norm_grads, block[:, width + 4 : width + 7]], axis=1).T
    mlp_pieces = lax.all_to_all(
        mlp_grad.reshape(MEMBERS, own_rows, -1), GROUP, 0, 0, tiled=True
    ).astype(FULL)
    mlp_grad = join_columns(mlp_pieces, 3)

    attn_new, attn_first_new, attn_second_new = adamw(
        attn_weight, attn_grad, attn_first, attn_second, rate_matrix, decay_matrix
    )
    mlp_new, mlp_first_new, mlp_second_new = adamw(
        mlp_weight, mlp_grad, mlp_first, mlp_second, rate_matrix, decay_matrix
    )
    small_new, small_first_new, small_second_new = adamw(
        small_weight, small_grad, small_first, small_second, rate_small, 0.0
    )
    return (
        output.astype(LOW),
        grad_tokens,
        attn_new,
        attn_first_new,
        attn_second_new,
        mlp_new,
        mlp_first_new,
        mlp_second_new,
        small_new,
        small_first_new,
        small_second_new,
    )


def solution(mesh):
    grid = Mesh(mesh.devices.reshape(4, 4, 4, 2), EVERY)
    rows, columns = (P(EVERY, None), P(None, EVERY))
    return jax.shard_map(
        local,
        mesh=grid,
        in_specs=(rows,) * 4 + (columns,) + (rows,) * 4 + (columns,) * 2,
        out_specs=(rows,) * 8 + (columns,) * 3,
        check_vma=False,
    )
```

```python
import functools

import jax
import jax.numpy as jnp
from jax import lax
from jax.experimental import pallas as pl
from jax.experimental.pallas import tpu as pltpu
from jax.sharding import Mesh, PartitionSpec as P

HEAD = 64
ROT = 16
STEP = 10

norm_eps = 1e-05
mask_fill = -1000000000.0
rope_base = 10000.0
beta_one = 0.9
beta_two = 0.95
adam_eps = 1e-08
rate_matrix = 0.01
rate_small = 0.1
decay_matrix = 0.1

LOW = jnp.bfloat16
FULL = jnp.float32

OUTER = ("y", "z")
GROUP = ("x", "core")
EVERY = OUTER + GROUP
RING = 4
MEMBERS = 8
OUTERS = 16


def product(left, right, dims):
    return lax.dot_general(left, right, (dims, ((), ())), preferred_element_type=FULL)


def normalize(values):
    center = values - jnp.mean(values, axis=-1, keepdims=True)
    spread = jnp.mean(center * center, axis=-1, keepdims=True)
    scaled = lax.rsqrt(spread + norm_eps)
    return (center * scaled, scaled)


def norm_back(grad_normed, normal, scaled, gain):
    grad_hat = grad_normed * gain
    return scaled * (
        grad_hat
        - jnp.mean(grad_hat, axis=-1, keepdims=True)
        - normal * jnp.mean(grad_hat * normal, axis=-1, keepdims=True)
    )


def rope_tables(rows, length, inner):
    half = ROT // 2
    lane = jnp.arange(inner) % HEAD
    position = (jnp.arange(rows) % length).astype(FULL)
    inverse = rope_base ** (-((lane % half).astype(FULL) * 2.0 / ROT))
    angle = position[:, None] * inverse[None, :]
    cosine = jnp.where(lane < ROT, jnp.cos(angle), 1.0)
    later = jnp.where(lane < half, -jnp.sin(angle), 0.0)
    earlier = jnp.where((lane >= half) & (lane < ROT), jnp.sin(angle), 0.0)
    return (cosine, later, earlier)


def rotate(values, tables, sign):
    cosine, later, earlier = tables
    half, lanes = (ROT // 2, values.shape[1])
    moved = pltpu.roll(values, lanes - half, 1) * later[...] + pltpu.roll(values, half, 1) * earlier[...]
    return values * cosine[...] + sign * moved


def pair_masks(length):
    rows = lax.broadcasted_iota(jnp.int32, (length, length), 0)
    columns = lax.broadcasted_iota(jnp.int32, (length, length), 1)
    lanes = lax.broadcasted_iota(jnp.int32, (length, 2 * HEAD), 1)
    return (rows >= columns, lanes < HEAD)


def soft(query, keyed, causal):
    scores = product(query, keyed, ((1,), (1,))) * HEAD**-0.5
    scores = jnp.where(causal, scores, mask_fill)
    weights = jnp.exp(scores - jnp.max(scores, axis=-1, keepdims=True))
    return weights / jnp.sum(weights, axis=-1, keepdims=True)


def out_columns(weights, inner, piece):
    start, step = (weights.shape[1] - inner, weights.shape[0] // OUTERS)
    rows = step // MEMBERS
    return jnp.concatenate(
        [weights[k * step + piece * rows : k * step + (piece + 1) * rows, start:] for k in range(OUTERS)], axis=0
    )


def attend_kernel(count, *refs):
    tokens, (weights, norm, bias, *tables) = (refs[:count], refs[count : count + 6])
    normed, turned, mixed, *branches = refs[count + 6 :]
    length, inner = (tokens[0].shape[0], bias.shape[1] // 3)
    causal, first = pair_masks(length)
    for block, part in enumerate(tokens):
        rows = slice(block * length, (block + 1) * length)
        normal, _ = normalize(part[...].astype(FULL))
        normed[rows] = (normal * norm[0:1] + norm[1:2]).astype(LOW)
    projected = product(normed[...], weights[:, : 3 * inner], ((1,), (0,))) + bias[...]
    for block in range(count):
        rows = slice(block * length, (block + 1) * length)
        query = rotate(projected[rows, :inner], tables, 1.0).astype(LOW)
        keyed = rotate(projected[rows, inner : 2 * inner], tables, 1.0).astype(LOW)
        valued = projected[rows, 2 * inner :].astype(LOW)
        turned[rows, :inner] = query
        turned[rows, inner : 2 * inner] = keyed
        turned[rows, 2 * inner :] = valued
        for column in range(0, inner, 2 * HEAD):
            at = slice(column, column + 2 * HEAD)
            outs = []
            for side in (first, ~first):
                prob = soft(jnp.where(side, query[:, at], 0), keyed[:, at], causal).astype(LOW)
                outs.append(product(prob, valued[:, at], ((1,), (0,))))
            mixed[rows, at] = jnp.where(first, outs[0], outs[1]).astype(LOW)
    half = length * count // 2
    for piece in range(MEMBERS):
        share = product(mixed[...], out_columns(weights, inner, piece), ((1,), (0,))).astype(LOW)
        for at, branch in enumerate(branches):
            branch[:, piece * inner : (piece + 1) * inner] = share[at * half : (at + 1) * half]


def attend(blocks, weights, norm, bias, tables):
    length, width = blocks[0].shape
    rows, inner = (length * len(blocks), bias.shape[1] // 3)
    shapes = ((rows, width), (rows, 3 * inner), (rows, inner), (rows // 2, width), (rows // 2, width))
    return pl.pallas_call(
        functools.partial(attend_kernel, len(blocks)),
        out_shape=[jax.ShapeDtypeStruct(shape, LOW) for shape in shapes],
        compiler_params=pltpu.CompilerParams(vmem_limit_bytes=28 << 20),
        cost_estimate=pl.CostEstimate(flops=10**9, bytes_accessed=rows * width, transcendentals=0),
        name="attend",
    )(*blocks, weights, norm, bias, *tables)


def attend_back_kernel(count, places, *refs):
    grads, tokens, refs = (refs[:count], refs[count : 2 * count], refs[2 * count :])
    weights, turned, sums_in, norm_in, *tables = refs[:7]
    back, sums, norm_sums, shares, back_mixed, normed_grad, low_grad, sent = refs[8:]
    length, inner = (grads[0].shape[0], turned.shape[1] // 3)
    total = 0.0
    for piece in range(MEMBERS):
        columns = slice(piece * inner, (piece + 1) * inner)
        rows = jnp.concatenate([grad[:, columns] for grad in grads], axis=0)
        total += product(rows, out_columns(weights, inner, piece), ((1,), (1,)))
    back_mixed[...] = total.astype(LOW)
    causal, first = pair_masks(length)
    bias_total = sums_in[...]
    for block in range(count):
        rows = slice(block * length, (block + 1) * length)
        parts = []
        for column in range(0, inner, 2 * HEAD):
            query, keyed, valued = (
                turned[rows, part * inner + column : part * inner + column + 2 * HEAD] for part in range(3)
            )
            grad_pair = back_mixed[rows, column : column + 2 * HEAD]
            back_query, back_key, back_value = ([], 0.0, 0.0)
            for side in (first, ~first):
                query_one = jnp.where(side, query, 0)
                grad_one = jnp.where(side, grad_pair, 0)
                prob = soft(query_one, keyed, causal)
                back_value += product(prob.astype(LOW), grad_one, ((0,), (0,)))
                grad_prob = product(grad_one, valued, ((1,), (1,)))
                delta = jnp.sum(prob * grad_prob, axis=-1, keepdims=True)
                grad_scores = (prob * (grad_prob - delta)).astype(LOW)
                back_query.append(product(grad_scores, keyed, ((1,), (0,))))
                back_key += product(grad_scores, query_one, ((0,), (0,)))
            back_query = jnp.where(first, back_query[0], back_query[1]) * HEAD**-0.5
            parts.append((back_query, back_key * HEAD**-0.5, back_value))
        back_query, back_key, back_value = (jnp.concatenate(side, axis=1) for side in zip(*parts))
        back[rows, :inner] = rotate(back_query, tables, -1.0).astype(LOW)
        back[rows, inner : 2 * inner] = rotate(back_key, tables, -1.0).astype(LOW)
        back[rows, 2 * inner :] = back_value.astype(LOW)
        bias_total += jnp.sum(back[rows].astype(FULL), axis=0, keepdims=True)
    sums[...] = bias_total
    normed_grad[...] = product(back[...], weights[:, : 3 * inner], ((1,), (1,)))
    scale_total, shift_total = (norm_in[0:8], norm_in[8:16])
    leaving = []
    for block in range(count):
        rows = slice(block * length, (block + 1) * length)
        low_grad[rows] = normed_grad[rows].astype(LOW)
        there = pl.ds(pl.multiple_of(places[block] * length, length), length)
        leaving.append(pltpu.make_async_copy(low_grad.at[rows], shares.at[there], sent.at[block]))
        leaving[-1].start()
    for block in range(count):
        rows = slice(block * length, (block + 1) * length)
        grad = normed_grad[rows]
        normal, _ = normalize(tokens[block][...].astype(FULL))
        scale_total += jnp.sum(grad * normal, axis=0, keepdims=True)
        shift_total += jnp.sum(grad, axis=0, keepdims=True)
    norm_sums[0:8] = scale_total
    norm_sums[8:16] = shift_total
    for copy in leaving:
        copy.wait()


def attend_back(places, grads, tokens, weights, turned, sums, norm_sums, shares, tables, micros):
    length, width = grads[0].shape
    count, (rows, columns) = (len(grads), turned.shape)
    made = (jax.ShapeDtypeStruct((rows, columns), LOW), sums, norm_sums, shares)
    operands = (places, *grads, *tokens, weights, turned, sums, norm_sums, *tables, shares)
    vmem, away = (pl.BlockSpec(memory_space=pltpu.VMEM), pl.BlockSpec(memory_space=pltpu.HBM))
    return pl.pallas_call(
        functools.partial(attend_back_kernel, count),
        in_specs=[pl.BlockSpec(memory_space=pltpu.SMEM)] + [vmem] * (len(operands) - 2) + [away],
        out_specs=[vmem] * 3 + [away],
        out_shape=[jax.ShapeDtypeStruct(m.shape, m.dtype) for m in made],
        scratch_shapes=[
            pltpu.VMEM((rows, columns // 3), LOW),
            pltpu.VMEM((rows, width), FULL),
            pltpu.VMEM((rows, width), LOW),
            pltpu.SemaphoreType.DMA((count,)),
        ],
        input_output_aliases={len(operands) - 1: 3},
        compiler_params=pltpu.CompilerParams(vmem_limit_bytes=28 << 20),
        cost_estimate=pl.CostEstimate(flops=micros * 10**9, bytes_accessed=rows * width, transcendentals=0),
        name="attend_back",
    )(*operands)


def residual_kernel(tokens, mine, arrived, twin, norm, residual, normed):
    total = tokens[...].astype(FULL) + mine[...].astype(FULL) + arrived[...].astype(FULL) + twin[...].astype(FULL)
    residual[...] = total
    normal, _ = normalize(total)
    normed[...] = (normal * norm[2:3] + norm[3:4]).astype(LOW)


def norm_back_kernel(given, row, low, values, base, *refs):
    grad = sum(g[...].astype(FULL) for g in refs[:given])
    norm, outs = (refs[given], refs[given + 1 :])
    normal, scaled = normalize(values[...].astype(FULL))
    total = base[...].astype(FULL) + norm_back(grad, normal, scaled, norm[row : row + 1])
    outs[0][...] = total
    if low:
        outs[1][...] = total.astype(LOW)

        @pl.when(pl.program_id(0) == 0)
        def _():
            outs[2][...] = jnp.zeros_like(outs[2])

        outs[2][0:8] += jnp.broadcast_to(jnp.sum(grad * normal, axis=0, keepdims=True), (8, grad.shape[1]))
        outs[2][8:16] += jnp.broadcast_to(jnp.sum(grad, axis=0, keepdims=True), (8, grad.shape[1]))


def by_rows(kernel, rows, operands, norm, shapes, name):
    block = rows // 4
    width = operands[0].shape[1]
    spot = pl.BlockSpec((block, width), lambda i: (i, 0))
    whole = [pl.BlockSpec(norm.shape, lambda i: (0, 0))] if norm is not None else []
    return pl.pallas_call(
        kernel,
        grid=(4,),
        in_specs=[spot] * len(operands) + whole,
        out_specs=[spot if shape[0] == rows else pl.BlockSpec(shape, lambda i: (0, 0)) for shape, _ in shapes],
        out_shape=[jax.ShapeDtypeStruct(shape, kind) for shape, kind in shapes],
        compiler_params=pltpu.CompilerParams(vmem_limit_bytes=16 << 20),
        cost_estimate=pl.CostEstimate(flops=10**8, bytes_accessed=10**6, transcendentals=0),
        name=name,
    )(*operands, *([norm] if whole else []))


def join_kernel(first, second, both):
    rows = first.shape[0]
    both[:rows] = first[...]
    both[rows:] = second[...]


def join_rows(first, second):
    rows, width = first.shape
    return pl.pallas_call(
        join_kernel,
        out_shape=jax.ShapeDtypeStruct((2 * rows, width), first.dtype),
        compiler_params=pltpu.CompilerParams(vmem_limit_bytes=8 << 20),
        cost_estimate=pl.CostEstimate(flops=1, bytes_accessed=1, transcendentals=0),
        name="join_rows",
    )(first, second)


def weight_grad_kernel(sizes, *refs):
    out, at, column = (refs[-1], 0, 0)
    for count in sizes:
        if count:
            lefts, rights = (refs[at : at + count[0]], refs[at + count[0] : at + sum(count)])
            total, rights = (0.0, list(rights))
            for left in lefts:
                right = [rights.pop(0)[...]]
                while sum(r.shape[0] for r in right) < left.shape[0]:
                    right.append(rights.pop(0)[...])
                total += product(left[...], jnp.concatenate(right, axis=0), ((0,), (0,)))
            at += sum(count)
        else:
            total = refs[at][...]
            if total.shape[0] == 8:
                total = jnp.concatenate([total, jnp.zeros((120, total.shape[1]), FULL)], axis=0).T
            at += 1
        out[:, column : column + total.shape[1]] = total.astype(LOW)
        column += total.shape[1]


def weight_grad(terms, block, limit):
    sizes, operands, specs, wide = ([], [], [], 0)
    for term in terms:
        if isinstance(term, tuple):
            lefts, rights = term
            height = lefts[0].shape[1]
            rows = min(block, height)
            columns = rights[0].shape[1]
            sizes.append((len(lefts), len(rights)))
            operands += [*lefts, *rights]
            specs += [pl.BlockSpec((left.shape[0], rows), lambda i: (0, i)) for left in lefts]
            specs += [pl.BlockSpec(right.shape, lambda i: (0, 0)) for right in rights]
        elif term.shape[0] == 8:
            columns = 128
            sizes.append(())
            operands.append(term)
            specs.append(pl.BlockSpec((8, rows), lambda i: (0, i)))
        else:
            columns = term.shape[1]
            sizes.append(())
            operands.append(term)
            specs.append(pl.BlockSpec((rows, columns), lambda i: (i, 0)))
        wide += columns
    return pl.pallas_call(
        functools.partial(weight_grad_kernel, tuple(sizes)),
        grid=(height // rows,),
        in_specs=specs,
        out_specs=pl.BlockSpec((rows, wide), lambda i: (i, 0)),
        out_shape=jax.ShapeDtypeStruct((height, wide), LOW),
        compiler_params=pltpu.CompilerParams(vmem_limit_bytes=limit << 20),
        cost_estimate=pl.CostEstimate(flops=height * wide, bytes_accessed=height * wide, transcendentals=0),
        name="weight_grad",
    )(*operands)


def adamw(weight, grad, first, second, rate, decay):
    first_new = beta_one * first + (1.0 - beta_one) * grad
    second_new = beta_two * second + (1.0 - beta_two) * grad * grad
    corr_one = 1.0 - beta_one**STEP
    corr_two = 1.0 - beta_two**STEP
    update = first_new / corr_one / (jnp.sqrt(second_new / corr_two) + adam_eps)
    return (weight - rate * (update + decay * weight), first_new, second_new)


def adamw_kernel(skip, pieces, weight, first, second, *outs):
    rows, wide = (weight.shape[0], weight.shape[1] // (pieces.shape[0] // 2))
    half = wide // 2
    across = -(-half // 128) * 128
    lanes = lax.broadcasted_iota(jnp.int32, (rows, wide), 1)
    blank = jnp.zeros((rows, wide - across), FULL)

    def turned(member, start, target):
        base = start // 128 * 128
        values = pieces[member, :, base : base + across].astype(FULL)
        move = (target - (start - base)) % across
        return pltpu.roll(values, move, 1) if move else values

    for part in range(3):

        @pl.when(pl.program_id(0) == part)
        def _():
            start = skip + part * half
            for pair in range(pieces.shape[0] // 2):
                left = jnp.concatenate([turned(2 * pair, start, 0), blank], axis=1)
                right = jnp.concatenate([blank, turned(2 * pair + 1, start, across - half)], axis=1)
                grad = jnp.where(lanes < half, left, right)
                at = (slice(None), slice(pair * wide, (pair + 1) * wide))
                made = adamw(weight[at], grad, first[at], second[at], rate_matrix, decay_matrix)
                for out, value in zip(outs, made):
                    out[at] = value


def adamw_mlp(pieces, skip, weight, first, second):
    rows, width = weight.shape
    spot = pl.BlockSpec((rows, width // 3), lambda part: (0, part))
    return pl.pallas_call(
        functools.partial(adamw_kernel, skip),
        grid=(3,),
        in_specs=[pl.BlockSpec(pieces.shape, lambda part: (0, 0, 0))] + [spot] * 3,
        out_specs=[spot] * 3,
        out_shape=[jax.ShapeDtypeStruct(weight.shape, FULL)] * 3,
        compiler_params=pltpu.CompilerParams(vmem_limit_bytes=24 << 20),
        cost_estimate=pl.CostEstimate(flops=10**8, bytes_accessed=7 * 4 * weight.size, transcendentals=0),
        name="adamw",
    )(pieces, weight, first, second)


def shift(values, axis, hop):
    return lax.ppermute(values, axis, [(i, (i + hop) % RING) for i in range(RING)])


def sibling(values):
    return lax.ppermute(values, "core", [(0, 1), (1, 0)])


def add(*values):
    return sum(v.astype(FULL) for v in values)


def hold(values, *others):
    return lax.optimization_barrier((values, others))[0]


def blocks_at(rows, places, length, column):
    width = rows.shape[1] // 2
    return [lax.dynamic_slice(rows, (place * length, column), (length, width)) for place in places]


def onward(values, back=False):
    moves = []
    for chip in range(RING):
        for core, hop in ((0, 1), (1, -1)):
            moves.append((2 * chip + core, 2 * ((chip + (-hop if back else hop)) % RING) + core))
    return lax.ppermute(values, GROUP, moves)


def group_places():
    chip, core = (lax.axis_index(axis) for axis in GROUP)
    one, two, far = ((chip + 3 + 2 * core) % RING, (chip + 1 + 2 * core) % RING, (chip + 2) % RING)
    other = 1 - core
    parts = (
        [2 * chip + core, 2 * chip + other],
        [2 * one + core, 2 * one + other, 2 * two + other, 2 * two + core],
        [2 * far + core, 2 * far + other],
    )
    return [jnp.stack(part).astype(jnp.int32) for part in parts]


def gather_group(values, work):
    rows = values.shape[0]
    own = join_rows(values, sibling(values))
    one = onward(own)
    parts = [[own[:rows], own[rows:]]]
    done = [work(0, parts[0])]
    one = hold(one, done[0][-1])
    far = onward(one[:rows])
    two = sibling(one)
    parts.append([one[:rows], one[rows:], two[:rows], two[rows:]])
    done.append(work(1, parts[1]))
    far = hold(far, done[1][-1])
    parts.append([far, sibling(far)])
    done.append(work(2, parts[2]))
    return (parts, done)


class Scatter:
    def far(self, blocks):
        self.sum = add(blocks[0], sibling(blocks[1])).astype(LOW)
        return self.sum

    def first(self):
        self.arrived = onward(self.sum, back=True)
        return self.arrived

    def near(self, blocks):
        self.both = add(blocks[0], sibling(blocks[1]))
        self.rows = self.both.shape[0] // 2
        return self.both

    def merge(self):
        rows = self.rows
        self.sum = jnp.concatenate([add(self.both[:rows], self.arrived), self.both[rows:]], axis=0).astype(LOW)
        return self.sum

    def second(self):
        self.arrived = onward(self.sum, back=True)
        return self.arrived

    def own(self, whole):
        rows = self.rows
        twin = sibling(add(whole[rows:], self.arrived[rows:]).astype(LOW))
        return (whole, self.arrived, twin)


def gather_outer(values):
    rows, columns = values.shape
    half = rows // 2
    place = {axis: lax.axis_index(axis) for axis in OUTER}

    def ring(block, axis, straight=False):
        before = shift(block, axis, 1)
        after = shift(block, axis, -1)
        if straight:
            return zip((block, before, after, shift(block, axis, 2)), [(place[axis] + j) % RING for j in (0, 3, 1, 2)], (0,) * 4)
        quarter = block.shape[0] // 2
        far = (shift(before[:quarter], axis, 1), shift(after[quarter:], axis, -1))
        spots = [(place[axis] + j) % RING for j in (0, 3, 1, 2, 2)]
        return zip((block, before, after, *far), spots, (0, 0, 0, 0, quarter))

    lines = []
    for axis, block in (("z", values[:half]), ("y", values[half:])):
        line = jnp.zeros((RING, half, columns), values.dtype)
        for piece, spot, start in ring(block, axis, True):
            line = lax.dynamic_update_slice(line, piece[None], (spot, start, 0))
        lines.append(line)
    whole = jnp.zeros((RING, RING, 2, half, columns), values.dtype)
    rings = [list(ring(line, axis)) for line, axis in zip(lines, ("y", "z"))]
    for piece, spot, start in rings[0]:
        whole = lax.dynamic_update_slice(whole, piece[None, :, None], (spot, start, 0, 0, 0))
    for piece, spot, start in rings[1]:
        whole = lax.dynamic_update_slice(whole, piece[:, None, None], (start, spot, 1, 0, 0))
    return whole.reshape(OUTERS * rows, columns)


def far_step(far, axis):
    half = far.shape[0] // 2
    return (shift(far[:half], axis, 1), shift(far[half:], axis, -1))


def near_shares(next_part, last_part, arrived):
    up, down = arrived
    half = up.shape[0]
    after = lax.dynamic_update_slice_in_dim(next_part, add(next_part[:half], up).astype(LOW), 0, 0)
    before = lax.dynamic_update_slice_in_dim(last_part, add(last_part[half:], down).astype(LOW), half, 0)
    return (after, before)


def near_step(shares, axis):
    return (shift(shares[0], axis, 1), shift(shares[1], axis, -1))


def reduce_ring(parts, axis):
    return add(parts[0], *(shift(parts[j], axis, j) for j in (1, 3, 2)))


def ring_order(values, axis, dim):
    place = lax.axis_index(axis)
    return [lax.dynamic_index_in_dim(values, (place + j) % RING, dim, keepdims=False) for j in range(RING)]


def block_moves(back):
    moves = []
    for outer in range(OUTERS):
        for member in range(MEMBERS):
            owner = member * OUTERS + outer
            here = outer * MEMBERS + member
            moves.append((here, owner) if back else (owner, here))
    return moves


def spread_columns(block, parts):
    rows = block.shape[0]
    return block.reshape(rows, parts, MEMBERS, -1).transpose(2, 0, 1, 3).reshape(MEMBERS, rows, -1)


def join_columns(pieces, parts):
    members, rows, width = pieces.shape
    turned = pieces.reshape(members, rows, parts, width // parts).transpose(1, 2, 0, 3)
    return turned.reshape(rows, members * width)


def local(
    tokens,
    cotangent,
    attn_weight,
    mlp_weight,
    small_weight,
    attn_first,
    attn_second,
    mlp_first,
    mlp_second,
    small_first,
    small_second,
):
    length, width = tokens.shape
    own_rows = attn_weight.shape[0]
    slab = own_rows * MEMBERS
    hidden = mlp_weight.shape[1] // 3 // MEMBERS
    inner = width // MEMBERS
    heads = inner // HEAD
    member = lax.axis_index(GROUP)

    rows_all = lax.all_gather(jnp.concatenate([tokens, cotangent], axis=1), GROUP, axis=0, tiled=True)

    attn_low = attn_weight.astype(LOW)
    small_low = jnp.pad(small_weight.astype(LOW).T, ((0, 0), (0, 121)))
    columns = 3 * inner + 128
    sent = jnp.concatenate(
        [
            spread_columns(attn_low[:, : 3 * width], 3),
            jnp.broadcast_to(small_low, (MEMBERS, own_rows, 128)),
            spread_columns(mlp_weight.astype(LOW), 3),
        ],
        axis=2,
    )
    slabs = lax.all_to_all(sent, GROUP, 0, 0, tiled=True).reshape(slab, columns + 3 * hidden)
    out_block = lax.ppermute(attn_low[:, 3 * width :], EVERY, block_moves(False))
    out_block = out_block.reshape(own_rows, MEMBERS, inner).transpose(1, 0, 2).reshape(slab, inner)
    mlp_part = lax.all_gather(slabs[:, columns:], OUTER, axis=0, tiled=True)
    places = group_places()
    tokens_all = [blocks_at(rows_all, part, length, 0) for part in places]
    attn_part = gather_outer(jnp.concatenate([slabs[:, :columns], out_block], axis=1))
    params = attn_part[:, 3 * inner : 3 * inner + 7].T.astype(FULL)
    bias = lax.dynamic_slice_in_dim(params[4:7], member * inner, inner, axis=1).reshape(1, -1)
    weight_wide = mlp_part[:, : 2 * hidden]
    weight_down = mlp_part[:, 2 * hidden :]

    tables = rope_tables(length, length, inner)
    cotangent_all = [jnp.concatenate(blocks_at(rows_all, part, length, width), axis=0) for part in places]

    def forward(blocks):
        return attend(blocks, attn_part, params[:2], bias, tables)

    ring = Scatter()
    kept = {2: forward(tokens_all[2])}
    ring.far(kept[2][3:])
    near_in = hold(tokens_all[1], ring.sum)
    ring.first()
    kept[1] = forward(near_in)
    ring.near(hold(kept[1][3:], ring.arrived))
    own_in, cotangent_all = hold((tokens_all[0], cotangent_all), ring.merge())
    own_in = hold(own_in, cotangent_all)
    ring.second()
    kept[0] = forward(own_in)
    ring.arrived = hold(ring.arrived, kept[0][3:])
    residual, normed_two = by_rows(
        residual_kernel,
        length,
        (tokens, kept[0][3], ring.arrived, sibling(add(kept[0][4], ring.arrived[length:]).astype(LOW))),
        params,
        (((length, width), FULL), ((length, width), LOW)),
        "residual",
    )
    normed_low, turned, mixed_low = ([kept[p][i] for p in range(3)] for i in range(3))

    def feed(part, blocks):
        rows = jnp.concatenate(blocks, axis=0)
        both = product(rows, weight_wide, ((1,), (0,)))
        gate, upward = (both[:, :hidden], both[:, hidden:])
        sigma = jax.nn.sigmoid(gate)
        active = gate * sigma
        hidden_low = (active * upward).astype(LOW)
        back_hidden = product(cotangent_all[part], weight_down, ((1,), (0,)))
        back_gate = (back_hidden * upward * sigma * (1.0 + gate * (1.0 - sigma))).astype(LOW)
        back_wide = jnp.concatenate([back_gate, (back_hidden * active).astype(LOW)], axis=1)
        share = product(back_wide, weight_wide, ((1,), (1,))).astype(LOW)
        return (rows, hidden_low, back_wide, share)

    def halves_of(rows):
        half = rows.shape[0] // 2
        return (rows[:half], rows[half:])

    def out_share(part):
        return product(hidden_low[part], weight_down, ((1,), (1,))).astype(LOW)

    _, done = gather_group(normed_two, feed)
    normed_two, hidden_low, back_wide, shares = (list(made) for made in zip(*done))
    ring = Scatter()
    ring.near(halves_of(shares[1]))
    ring.far(halves_of(shares[2]))
    hidden_low = hold(hidden_low, ring.sum)
    ring.first()
    out_shares = [out_share(part) for part in range(3)]
    ring.arrived = hold(ring.arrived, out_shares)
    ring.merge()
    back_wide = hold(back_wide, ring.sum)
    ring.second()
    mlp_grad = weight_grad([(normed_two, back_wide), (cotangent_all, hidden_low)], 512, 36)
    ring.arrived = hold(ring.arrived, mlp_grad)
    back_residual, back_low, norm_two_grads = by_rows(
        functools.partial(norm_back_kernel, 3, 2, True),
        length,
        (residual, cotangent, *ring.own(shares[0])),
        params,
        (((length, width), FULL), ((length, width), LOW), ((16, width), FULL)),
        "norm_back",
    )
    mlp_grad = lax.psum_scatter(mlp_grad, OUTER, scatter_dimension=0, tiled=True)

    back_sums = [jnp.zeros((8, 3 * inner), FULL), jnp.zeros((16, width), FULL), jnp.zeros((MEMBERS * length, width), LOW)]
    ring = Scatter()
    taken, out_grads = ([], [])

    def out_grad():
        grad = weight_grad([(mixed_low, taken)], inner, 16)
        grad = grad.reshape(OUTERS, own_rows, MEMBERS, inner).transpose(0, 2, 1, 3)
        return grad.reshape(width, inner)

    def backward(part, blocks):
        if part == 1:
            ring.far(hold(halves_of(out_shares[2]), blocks[0]))
            blocks = hold(blocks, ring.sum)
            ring.first()
        elif part == 2:
            ring.near(halves_of(out_shares[1]))
            blocks = hold(blocks, ring.merge())
            ring.second()
        taken.extend(blocks)
        if part == 2:
            out_grads[:] = [out_grad()]
            blocks = hold(blocks, out_grads)
        made = attend_back(
            places[part], blocks, tokens_all[part], attn_part, turned[part], *back_sums, tables, (20, 40, 20)[part]
        )
        back_sums[:] = made[1:]
        return made[:2]

    _, done = gather_group(back_low, backward)
    back_proj = [made[0] for made in done]

    bias_rows = jnp.pad(
        back_sums[0][0].reshape(3, OUTERS, own_rows), ((0, 0), (0, 0), (0, slab - own_rows))
    ).reshape(3, width)
    small_rows = jnp.concatenate(
        [
            back_sums[1][:1],
            back_sums[1][8:9],
            norm_two_grads[:1],
            norm_two_grads[8:9],
            bias_rows,
            jnp.zeros((1, width), FULL),
        ],
        axis=0,
    )
    back_proj = hold(back_proj, ring.arrived)
    attn_grad = weight_grad([(normed_low, back_proj), small_rows, out_grads[0]], 512, 60)
    output = add(residual, *(rows[:length] for rows in ring.own(hold(out_shares[0], attn_grad))))
    blocks = attn_grad.reshape(RING, RING, 2, slab // 2, -1)
    parts = [ring_order(blocks[:, :, half], axis, half) for half, axis in enumerate(OUTER)]
    arrived = [far_step(part[2], axis) for part, axis in zip(parts, OUTER)]
    shares = [near_shares(part[1], part[3], halves) for part, halves in zip(parts, arrived)]
    totals = [
        add(part[0], *near_step(share, axis)).astype(LOW) for part, share, axis in zip(parts, shares, OUTER)
    ]
    back_normed_one = lax.psum_scatter(hold(back_sums[2], shares), GROUP, scatter_dimension=0, tiled=True)
    totals = hold(totals, mlp_grad, output)
    totals = [reduce_ring(ring_order(total, axis, 0), axis).astype(LOW) for total, axis in zip(totals, OUTER[::-1])]
    attn_grad = hold(jnp.concatenate(totals, axis=0), back_normed_one)
    (grad_tokens,) = by_rows(
        functools.partial(norm_back_kernel, 1, 0, False),
        length,
        (tokens, back_residual, back_normed_one),
        params,
        (((length, width), FULL),),
        "norm_back",
    )
    out_grad = (
        attn_grad[:, 3 * inner + 128 :]
        .reshape(MEMBERS, own_rows, inner)
        .transpose(1, 0, 2)
        .reshape(own_rows, width)
    )
    bias_grad = attn_grad[:own_rows, 3 * inner : 3 * inner + 128]
    block = lax.ppermute(
        jnp.concatenate([out_grad, bias_grad], axis=1), EVERY, block_moves(True)
    ).astype(FULL)
    blank = jnp.zeros((slab, -(columns + 3 * hidden) % 128), LOW)
    pieces = jnp.concatenate([attn_grad[:, :columns], mlp_grad, blank], axis=1).reshape(MEMBERS, own_rows, -1)
    all_pieces = lax.all_to_all(pieces, GROUP, 0, 0, tiled=True)
    pieces = all_pieces[:, :, :columns].astype(FULL)
    attn_grad = jnp.concatenate(
        [join_columns(pieces[:, :, : 3 * inner], 3), block[:, :width]], axis=1
    )
    norm_grads = jnp.sum(pieces[:, :, 3 * inner : 3 * inner + 4], axis=0)
    small_grad = jnp.concatenate([norm_grads, block[:, width + 4 : width + 7]], axis=1).T

    attn_new, attn_first_new, attn_second_new = adamw(
        attn_weight, attn_grad, attn_first, attn_second, rate_matrix, decay_matrix
    )
    mlp_new, mlp_first_new, mlp_second_new = adamw_mlp(all_pieces, columns, mlp_weight, mlp_first, mlp_second)
    small_new, small_first_new, small_second_new = adamw(
        small_weight, small_grad, small_first, small_second, rate_small, 0.0
    )
    return (
        output.astype(LOW),
        grad_tokens,
        attn_new,
        attn_first_new,
        attn_second_new,
        mlp_new,
        mlp_first_new,
        mlp_second_new,
        small_new,
        small_first_new,
        small_second_new,
    )


def solution(mesh):
    grid = Mesh(mesh.devices.reshape(4, 4, 4, 2), EVERY)
    rows, columns = (P(EVERY, None), P(None, EVERY))
    return jax.shard_map(
        local,
        mesh=grid,
        in_specs=(rows,) * 4 + (columns,) + (rows,) * 4 + (columns,) * 2,
        out_specs=(rows,) * 8 + (columns,) * 3,
        check_vma=False,
    )
```

```python
import functools

import jax
import jax.numpy as jnp
from jax import lax
from jax.experimental import pallas as pl
from jax.experimental.pallas import tpu as pltpu
from jax.sharding import Mesh, PartitionSpec as P

HEAD = 64
ROT = 16
STEP = 10

norm_eps = 1e-05
mask_fill = -1000000000.0
rope_base = 10000.0
beta_one = 0.9
beta_two = 0.95
adam_eps = 1e-08
rate_matrix = 0.01
rate_small = 0.1
decay_matrix = 0.1

LOW = jnp.bfloat16
FULL = jnp.float32

OUTER = ("y", "z")
GROUP = ("x", "core")
EVERY = OUTER + GROUP
RING = 4
MEMBERS = 8
OUTERS = 16


def product(left, right, dims):
    return lax.dot_general(left, right, (dims, ((), ())), preferred_element_type=FULL)


def normalize(values):
    center = values - jnp.mean(values, axis=-1, keepdims=True)
    spread = jnp.mean(center * center, axis=-1, keepdims=True)
    scaled = lax.rsqrt(spread + norm_eps)
    return (center * scaled, scaled)


def norm_back(grad_normed, normal, scaled, gain):
    grad_hat = grad_normed * gain
    return scaled * (
        grad_hat
        - jnp.mean(grad_hat, axis=-1, keepdims=True)
        - normal * jnp.mean(grad_hat * normal, axis=-1, keepdims=True)
    )


def rope_tables(rows, length, inner):
    half = ROT // 2
    lane = jnp.arange(inner) % HEAD
    position = (jnp.arange(rows) % length).astype(FULL)
    inverse = rope_base ** (-((lane % half).astype(FULL) * 2.0 / ROT))
    angle = position[:, None] * inverse[None, :]
    cosine = jnp.where(lane < ROT, jnp.cos(angle), 1.0)
    later = jnp.where(lane < half, -jnp.sin(angle), 0.0)
    earlier = jnp.where((lane >= half) & (lane < ROT), jnp.sin(angle), 0.0)
    return (cosine, later, earlier)


def rotate(values, tables, sign):
    cosine, later, earlier = tables
    half, lanes = (ROT // 2, values.shape[1])
    moved = pltpu.roll(values, lanes - half, 1) * later[...] + pltpu.roll(values, half, 1) * earlier[...]
    return values * cosine[...] + sign * moved


def pair_masks(length):
    rows = lax.broadcasted_iota(jnp.int32, (length, length), 0)
    columns = lax.broadcasted_iota(jnp.int32, (length, length), 1)
    lanes = lax.broadcasted_iota(jnp.int32, (length, 2 * HEAD), 1)
    return (rows >= columns, lanes < HEAD)


def soft(query, keyed, causal):
    scores = product(query, keyed, ((1,), (1,))) * HEAD**-0.5
    scores = jnp.where(causal, scores, mask_fill)
    weights = jnp.exp(scores - jnp.max(scores, axis=-1, keepdims=True))
    return weights / jnp.sum(weights, axis=-1, keepdims=True)


def out_columns(weights, inner, piece):
    start, step = (weights.shape[1] - inner, weights.shape[0] // OUTERS)
    rows = step // MEMBERS
    return jnp.concatenate(
        [weights[k * step + piece * rows : k * step + (piece + 1) * rows, start:] for k in range(OUTERS)], axis=0
    )


def attend_kernel(count, *refs):
    tokens, (weights, norm, bias, *tables) = (refs[:count], refs[count : count + 6])
    normed, turned, mixed, *branches = refs[count + 6 :]
    length, inner = (tokens[0].shape[0], bias.shape[1] // 3)
    causal, first = pair_masks(length)
    for block, part in enumerate(tokens):
        rows = slice(block * length, (block + 1) * length)
        normal, _ = normalize(part[...].astype(FULL))
        normed[rows] = (normal * norm[0:1] + norm[1:2]).astype(LOW)
    projected = product(normed[...], weights[:, : 3 * inner], ((1,), (0,))) + bias[...]
    for block in range(count):
        rows = slice(block * length, (block + 1) * length)
        query = rotate(projected[rows, :inner], tables, 1.0).astype(LOW)
        keyed = rotate(projected[rows, inner : 2 * inner], tables, 1.0).astype(LOW)
        valued = projected[rows, 2 * inner :].astype(LOW)
        turned[rows, :inner] = query
        turned[rows, inner : 2 * inner] = keyed
        turned[rows, 2 * inner :] = valued
        for column in range(0, inner, 2 * HEAD):
            at = slice(column, column + 2 * HEAD)
            outs = []
            for side in (first, ~first):
                prob = soft(jnp.where(side, query[:, at], 0), keyed[:, at], causal).astype(LOW)
                outs.append(product(prob, valued[:, at], ((1,), (0,))))
            mixed[rows, at] = jnp.where(first, outs[0], outs[1]).astype(LOW)
    half = length * count // 2
    for piece in range(MEMBERS):
        share = product(mixed[...], out_columns(weights, inner, piece), ((1,), (0,))).astype(LOW)
        for at, branch in enumerate(branches):
            branch[:, piece * inner : (piece + 1) * inner] = share[at * half : (at + 1) * half]


def attend(blocks, weights, norm, bias, tables):
    length, width = blocks[0].shape
    rows, inner = (length * len(blocks), bias.shape[1] // 3)
    shapes = ((rows, width), (rows, 3 * inner), (rows, inner), (rows // 2, width), (rows // 2, width))
    return pl.pallas_call(
        functools.partial(attend_kernel, len(blocks)),
        out_shape=[jax.ShapeDtypeStruct(shape, LOW) for shape in shapes],
        compiler_params=pltpu.CompilerParams(vmem_limit_bytes=28 << 20),
        cost_estimate=pl.CostEstimate(flops=10**9, bytes_accessed=rows * width, transcendentals=0),
        name="attend",
    )(*blocks, weights, norm, bias, *tables)


def attend_back_kernel(count, places, *refs):
    grads, tokens, refs = (refs[:count], refs[count : 2 * count], refs[2 * count :])
    weights, turned, sums_in, norm_in, *tables = refs[:7]
    back, sums, norm_sums, shares, back_mixed, normed_grad, low_grad, sent = refs[8:]
    length, inner = (grads[0].shape[0], turned.shape[1] // 3)
    total = 0.0
    for piece in range(MEMBERS):
        columns = slice(piece * inner, (piece + 1) * inner)
        rows = jnp.concatenate([grad[:, columns] for grad in grads], axis=0)
        total += product(rows, out_columns(weights, inner, piece), ((1,), (1,)))
    back_mixed[...] = total.astype(LOW)
    causal, first = pair_masks(length)
    bias_total = sums_in[...]
    for block in range(count):
        rows = slice(block * length, (block + 1) * length)
        parts = []
        for column in range(0, inner, 2 * HEAD):
            query, keyed, valued = (
                turned[rows, part * inner + column : part * inner + column + 2 * HEAD] for part in range(3)
            )
            grad_pair = back_mixed[rows, column : column + 2 * HEAD]
            back_query, back_key, back_value = ([], 0.0, 0.0)
            for side in (first, ~first):
                query_one = jnp.where(side, query, 0)
                grad_one = jnp.where(side, grad_pair, 0)
                prob = soft(query_one, keyed, causal)
                back_value += product(prob.astype(LOW), grad_one, ((0,), (0,)))
                grad_prob = product(grad_one, valued, ((1,), (1,)))
                delta = jnp.sum(prob * grad_prob, axis=-1, keepdims=True)
                grad_scores = (prob * (grad_prob - delta)).astype(LOW)
                back_query.append(product(grad_scores, keyed, ((1,), (0,))))
                back_key += product(grad_scores, query_one, ((0,), (0,)))
            back_query = jnp.where(first, back_query[0], back_query[1]) * HEAD**-0.5
            parts.append((back_query, back_key * HEAD**-0.5, back_value))
        back_query, back_key, back_value = (jnp.concatenate(side, axis=1) for side in zip(*parts))
        back[rows, :inner] = rotate(back_query, tables, -1.0).astype(LOW)
        back[rows, inner : 2 * inner] = rotate(back_key, tables, -1.0).astype(LOW)
        back[rows, 2 * inner :] = back_value.astype(LOW)
        bias_total += jnp.sum(back[rows].astype(FULL), axis=0, keepdims=True)
    sums[...] = bias_total
    normed_grad[...] = product(back[...], weights[:, : 3 * inner], ((1,), (1,)))
    scale_total, shift_total = (norm_in[0:8], norm_in[8:16])
    leaving = []
    for block in range(count):
        rows = slice(block * length, (block + 1) * length)
        low_grad[rows] = normed_grad[rows].astype(LOW)
        there = pl.ds(pl.multiple_of(places[block] * length, length), length)
        leaving.append(pltpu.make_async_copy(low_grad.at[rows], shares.at[there], sent.at[block]))
        leaving[-1].start()
    for block in range(count):
        rows = slice(block * length, (block + 1) * length)
        grad = normed_grad[rows]
        normal, _ = normalize(tokens[block][...].astype(FULL))
        scale_total += jnp.sum(grad * normal, axis=0, keepdims=True)
        shift_total += jnp.sum(grad, axis=0, keepdims=True)
    norm_sums[0:8] = scale_total
    norm_sums[8:16] = shift_total
    for copy in leaving:
        copy.wait()


def attend_back(places, grads, tokens, weights, turned, sums, norm_sums, shares, tables, micros):
    length, width = grads[0].shape
    count, (rows, columns) = (len(grads), turned.shape)
    made = (jax.ShapeDtypeStruct((rows, columns), LOW), sums, norm_sums, shares)
    operands = (places, *grads, *tokens, weights, turned, sums, norm_sums, *tables, shares)
    vmem, away = (pl.BlockSpec(memory_space=pltpu.VMEM), pl.BlockSpec(memory_space=pltpu.HBM))
    return pl.pallas_call(
        functools.partial(attend_back_kernel, count),
        in_specs=[pl.BlockSpec(memory_space=pltpu.SMEM)] + [vmem] * (len(operands) - 2) + [away],
        out_specs=[vmem] * 3 + [away],
        out_shape=[jax.ShapeDtypeStruct(m.shape, m.dtype) for m in made],
        scratch_shapes=[
            pltpu.VMEM((rows, columns // 3), LOW),
            pltpu.VMEM((rows, width), FULL),
            pltpu.VMEM((rows, width), LOW),
            pltpu.SemaphoreType.DMA((count,)),
        ],
        input_output_aliases={len(operands) - 1: 3},
        compiler_params=pltpu.CompilerParams(vmem_limit_bytes=28 << 20),
        cost_estimate=pl.CostEstimate(flops=micros * 10**9, bytes_accessed=rows * width, transcendentals=0),
        name="attend_back",
    )(*operands)


def residual_kernel(tokens, mine, arrived, twin, norm, residual, normed):
    total = tokens[...].astype(FULL) + mine[...].astype(FULL) + arrived[...].astype(FULL) + twin[...].astype(FULL)
    residual[...] = total
    normal, _ = normalize(total)
    normed[...] = (normal * norm[2:3] + norm[3:4]).astype(LOW)


def norm_back_kernel(given, row, low, values, base, *refs):
    grad = sum(g[...].astype(FULL) for g in refs[:given])
    norm, outs = (refs[given], refs[given + 1 :])
    normal, scaled = normalize(values[...].astype(FULL))
    total = base[...].astype(FULL) + norm_back(grad, normal, scaled, norm[row : row + 1])
    outs[0][...] = total
    if low:
        outs[1][...] = total.astype(LOW)

        @pl.when(pl.program_id(0) == 0)
        def _():
            outs[2][...] = jnp.zeros_like(outs[2])

        outs[2][0:8] += jnp.broadcast_to(jnp.sum(grad * normal, axis=0, keepdims=True), (8, grad.shape[1]))
        outs[2][8:16] += jnp.broadcast_to(jnp.sum(grad, axis=0, keepdims=True), (8, grad.shape[1]))


def by_rows(kernel, rows, operands, norm, shapes, name):
    block = rows // 2
    width = operands[0].shape[1]
    spot = pl.BlockSpec((block, width), lambda i: (i, 0))
    whole = [pl.BlockSpec(norm.shape, lambda i: (0, 0))] if norm is not None else []
    return pl.pallas_call(
        kernel,
        grid=(rows // block,),
        in_specs=[spot] * len(operands) + whole,
        out_specs=[spot if shape[0] == rows else pl.BlockSpec(shape, lambda i: (0, 0)) for shape, _ in shapes],
        out_shape=[jax.ShapeDtypeStruct(shape, kind) for shape, kind in shapes],
        compiler_params=pltpu.CompilerParams(vmem_limit_bytes=16 << 20),
        cost_estimate=pl.CostEstimate(flops=10**8, bytes_accessed=10**6, transcendentals=0),
        name=name,
    )(*operands, *([norm] if whole else []))


def join_kernel(first, second, both):
    rows = first.shape[0]
    both[:rows] = first[...]
    both[rows:] = second[...]


def join_rows(first, second):
    rows, width = first.shape
    return pl.pallas_call(
        join_kernel,
        out_shape=jax.ShapeDtypeStruct((2 * rows, width), first.dtype),
        compiler_params=pltpu.CompilerParams(vmem_limit_bytes=8 << 20),
        cost_estimate=pl.CostEstimate(flops=1, bytes_accessed=1, transcendentals=0),
        name="join_rows",
    )(first, second)


def weight_grad_kernel(sizes, *refs):
    out, at, column = (refs[-1], 0, 0)
    for count in sizes:
        if count:
            lefts, rights = (refs[at : at + count[0]], refs[at + count[0] : at + sum(count)])
            total, rights = (0.0, list(rights))
            for left in lefts:
                right = [rights.pop(0)[...]]
                while sum(r.shape[0] for r in right) < left.shape[0]:
                    right.append(rights.pop(0)[...])
                total += product(left[...], jnp.concatenate(right, axis=0), ((0,), (0,)))
            at += sum(count)
        else:
            total = refs[at][...]
            if total.shape[0] == 8:
                total = jnp.concatenate([total, jnp.zeros((120, total.shape[1]), FULL)], axis=0).T
            at += 1
        out[:, column : column + total.shape[1]] = total.astype(LOW)
        column += total.shape[1]


def weight_grad(terms, block, limit):
    sizes, operands, specs, wide = ([], [], [], 0)
    for term in terms:
        if isinstance(term, tuple):
            lefts, rights = term
            height = lefts[0].shape[1]
            rows = min(block, height)
            columns = rights[0].shape[1]
            sizes.append((len(lefts), len(rights)))
            operands += [*lefts, *rights]
            specs += [pl.BlockSpec((left.shape[0], rows), lambda i: (0, i)) for left in lefts]
            specs += [pl.BlockSpec(right.shape, lambda i: (0, 0)) for right in rights]
        elif term.shape[0] == 8:
            columns = 128
            sizes.append(())
            operands.append(term)
            specs.append(pl.BlockSpec((8, rows), lambda i: (0, i)))
        else:
            columns = term.shape[1]
            sizes.append(())
            operands.append(term)
            specs.append(pl.BlockSpec((rows, columns), lambda i: (i, 0)))
        wide += columns
    return pl.pallas_call(
        functools.partial(weight_grad_kernel, tuple(sizes)),
        grid=(height // rows,),
        in_specs=specs,
        out_specs=pl.BlockSpec((rows, wide), lambda i: (i, 0)),
        out_shape=jax.ShapeDtypeStruct((height, wide), LOW),
        compiler_params=pltpu.CompilerParams(vmem_limit_bytes=limit << 20),
        cost_estimate=pl.CostEstimate(flops=height * wide, bytes_accessed=height * wide, transcendentals=0),
        name="weight_grad",
    )(*operands)


def attn_grad_kernel(count, place, *refs):
    lefts, rights = (refs[:count], refs[count : 2 * count])
    one, two, bias, packed, first, second = refs[2 * count :]
    grad = 0.0
    for left, right in zip(lefts, rights):
        grad += product(left[...], right[...], ((0,), (0,)))
    columns, rows = (grad.shape[1], grad.shape[0] // RING)
    small = jnp.concatenate([one[0:1], one[8:9], two[0:1], two[8:9], bias[0:4]], axis=0)
    small = jnp.concatenate([small, jnp.zeros((120, small.shape[1]), FULL)], axis=0).T
    for z in range(RING):
        spot = lax.rem(z + RING - place[1], RING)
        for half, (out, at) in enumerate(((first, (0, spot)), (second, (spot, 0)))):
            here = slice(z * rows + half * rows // 2, z * rows + (half + 1) * rows // 2)
            out[(*at, slice(None), slice(0, columns))] = grad[here].astype(LOW)
            out[(*at, slice(None), slice(columns, columns + 128))] = small[here].astype(LOW)
            out[(*at, slice(None), slice(columns + 128, None))] = packed[here]


def attn_grads(lefts, rights, norm_one, norm_two, bias, packed):
    width, columns = (lefts[0].shape[1], rights[0].shape[1])
    wide, rows = (columns + 128 + packed.shape[1], width // RING)
    place = jnp.stack([lax.axis_index(axis) for axis in OUTER]).astype(jnp.int32)
    half = rows // RING // 2

    def here(j, place):
        return lax.rem(place[0] + j, RING)

    return pl.pallas_call(
        functools.partial(attn_grad_kernel, len(lefts)),
        grid_spec=pltpu.PrefetchScalarGridSpec(
            num_scalar_prefetch=1,
            grid=(RING,),
            in_specs=[pl.BlockSpec((left.shape[0], rows), lambda j, place: (0, here(j, place))) for left in lefts]
            + [pl.BlockSpec(right.shape, lambda j, place: (0, 0)) for right in rights]
            + [pl.BlockSpec((a.shape[0], rows), lambda j, place: (0, here(j, place))) for a in (norm_one, norm_two, bias)]
            + [pl.BlockSpec((rows, packed.shape[1]), lambda j, place: (here(j, place), 0))],
            out_specs=[
                pl.BlockSpec((1, RING, half, wide), lambda j, place: (j, 0, 0, 0)),
                pl.BlockSpec((RING, 1, half, wide), lambda j, place: (0, j, 0, 0)),
            ],
        ),
        out_shape=[jax.ShapeDtypeStruct((RING, RING, half, wide), LOW)] * 2,
        compiler_params=pltpu.CompilerParams(vmem_limit_bytes=60 << 20),
        cost_estimate=pl.CostEstimate(flops=10**9, bytes_accessed=10**6, transcendentals=0),
        name="attn_grads",
    )(place, *lefts, *rights, norm_one, norm_two, bias, packed)


def adamw(weight, grad, first, second, rate, decay):
    first_new = beta_one * first + (1.0 - beta_one) * grad
    second_new = beta_two * second + (1.0 - beta_two) * grad * grad
    corr_one = 1.0 - beta_one**STEP
    corr_two = 1.0 - beta_two**STEP
    update = first_new / corr_one / (jnp.sqrt(second_new / corr_two) + adam_eps)
    return (weight - rate * (update + decay * weight), first_new, second_new)


def adamw_kernel(skip, pieces, weight, first, second, *outs):
    rows, wide = (weight.shape[0], weight.shape[1] // (pieces.shape[0] // 2))
    half = wide // 2
    across = -(-half // 128) * 128
    lanes = lax.broadcasted_iota(jnp.int32, (rows, wide), 1)
    blank = jnp.zeros((rows, wide - across), FULL)

    def turned(member, start, target):
        base = start // 128 * 128
        values = pieces[member, :, base : base + across].astype(FULL)
        move = (target - (start - base)) % across
        return pltpu.roll(values, move, 1) if move else values

    for part in range(3):

        @pl.when(pl.program_id(0) == part)
        def _():
            start = skip + part * half
            for pair in range(pieces.shape[0] // 2):
                left = jnp.concatenate([turned(2 * pair, start, 0), blank], axis=1)
                right = jnp.concatenate([blank, turned(2 * pair + 1, start, across - half)], axis=1)
                grad = jnp.where(lanes < half, left, right)
                at = (slice(None), slice(pair * wide, (pair + 1) * wide))
                made = adamw(weight[at], grad, first[at], second[at], rate_matrix, decay_matrix)
                for out, value in zip(outs, made):
                    out[at] = value


def adamw_mlp(pieces, skip, weight, first, second):
    rows, width = weight.shape
    spot = pl.BlockSpec((rows, width // 3), lambda part: (0, part))
    return pl.pallas_call(
        functools.partial(adamw_kernel, skip),
        grid=(3,),
        in_specs=[pl.BlockSpec(pieces.shape, lambda part: (0, 0, 0))] + [spot] * 3,
        out_specs=[spot] * 3,
        out_shape=[jax.ShapeDtypeStruct(weight.shape, FULL)] * 3,
        compiler_params=pltpu.CompilerParams(vmem_limit_bytes=24 << 20),
        cost_estimate=pl.CostEstimate(flops=10**8, bytes_accessed=7 * 4 * weight.size, transcendentals=0),
        name="adamw",
    )(pieces, weight, first, second)


def shift(values, axis, hop):
    return lax.ppermute(values, axis, [(i, (i + hop) % RING) for i in range(RING)])


def sibling(values):
    return lax.ppermute(values, "core", [(0, 1), (1, 0)])


def add(*values):
    return sum(v.astype(FULL) for v in values)


def hold(values, *others):
    return lax.optimization_barrier((values, others))[0]


def blocks_at(rows, places, length, column):
    width = rows.shape[1] // 2
    return [lax.dynamic_slice(rows, (place * length, column), (length, width)) for place in places]


def onward(values, back=False):
    moves = []
    for chip in range(RING):
        for core, hop in ((0, 1), (1, -1)):
            moves.append((2 * chip + core, 2 * ((chip + (-hop if back else hop)) % RING) + core))
    return lax.ppermute(values, GROUP, moves)


def group_places():
    chip, core = (lax.axis_index(axis) for axis in GROUP)
    one, two, far = ((chip + 3 + 2 * core) % RING, (chip + 1 + 2 * core) % RING, (chip + 2) % RING)
    other = 1 - core
    parts = (
        [2 * chip + core, 2 * chip + other],
        [2 * one + core, 2 * one + other, 2 * two + other, 2 * two + core],
        [2 * far + core, 2 * far + other],
    )
    return [jnp.stack(part).astype(jnp.int32) for part in parts]


def gather_group(values, work):
    rows = values.shape[0]
    own = join_rows(values, sibling(values))
    one = onward(own)
    parts = [[own[:rows], own[rows:]]]
    done = [work(0, parts[0])]
    one = hold(one, done[0][-1])
    far = onward(one[:rows])
    two = sibling(one)
    parts.append([one[:rows], one[rows:], two[:rows], two[rows:]])
    done.append(work(1, parts[1]))
    far = hold(far, done[1][-1])
    parts.append([far, sibling(far)])
    done.append(work(2, parts[2]))
    return (parts, done)


class Scatter:
    def far(self, blocks):
        self.sum = add(blocks[0], sibling(blocks[1])).astype(LOW)
        return self.sum

    def first(self):
        self.arrived = onward(self.sum, back=True)
        return self.arrived

    def near(self, blocks):
        self.both = add(blocks[0], sibling(blocks[1]))
        self.rows = self.both.shape[0] // 2
        return self.both

    def merge(self):
        rows = self.rows
        self.sum = jnp.concatenate([add(self.both[:rows], self.arrived), self.both[rows:]], axis=0).astype(LOW)
        return self.sum

    def second(self):
        self.arrived = onward(self.sum, back=True)
        return self.arrived

    def own(self, whole):
        rows = self.rows
        twin = sibling(add(whole[rows:], self.arrived[rows:]).astype(LOW))
        return (whole, self.arrived, twin)


def gather_outer(values):
    rows, columns = values.shape
    half = rows // 2
    place = {axis: lax.axis_index(axis) for axis in OUTER}

    def ring(block, axis, straight=False):
        before = shift(block, axis, 1)
        after = shift(block, axis, -1)
        if straight:
            return zip((block, before, after, shift(block, axis, 2)), [(place[axis] + j) % RING for j in (0, 3, 1, 2)], (0,) * 4)
        quarter = block.shape[0] // 2
        far = (shift(before[:quarter], axis, 1), shift(after[quarter:], axis, -1))
        spots = [(place[axis] + j) % RING for j in (0, 3, 1, 2, 2)]
        return zip((block, before, after, *far), spots, (0, 0, 0, 0, quarter))

    lines = []
    for axis, block in (("z", values[:half]), ("y", values[half:])):
        line = jnp.zeros((RING, half, columns), values.dtype)
        for piece, spot, start in ring(block, axis, True):
            line = lax.dynamic_update_slice(line, piece[None], (spot, start, 0))
        lines.append(line)
    whole = jnp.zeros((RING, RING, 2, half, columns), values.dtype)
    rings = [list(ring(line, axis)) for line, axis in zip(lines, ("y", "z"))]
    for piece, spot, start in rings[0]:
        whole = lax.dynamic_update_slice(whole, piece[None, :, None], (spot, start, 0, 0, 0))
    for piece, spot, start in rings[1]:
        whole = lax.dynamic_update_slice(whole, piece[:, None, None], (start, spot, 1, 0, 0))
    return whole.reshape(OUTERS * rows, columns)


def far_step(far, axis):
    half = far.shape[0] // 2
    return (shift(far[:half], axis, 1), shift(far[half:], axis, -1))


def near_shares(next_part, last_part, arrived):
    up, down = arrived
    half = up.shape[0]
    after = lax.dynamic_update_slice_in_dim(next_part, add(next_part[:half], up).astype(LOW), 0, 0)
    before = lax.dynamic_update_slice_in_dim(last_part, add(last_part[half:], down).astype(LOW), half, 0)
    return (after, before)


def near_step(shares, axis):
    return (shift(shares[0], axis, 1), shift(shares[1], axis, -1))


def reduce_ring(parts, axis):
    return add(parts[0], *(shift(parts[j], axis, j) for j in (1, 3, 2)))


def ring_order(values, axis, dim):
    place = lax.axis_index(axis)
    return [lax.dynamic_index_in_dim(values, (place + j) % RING, dim, keepdims=False) for j in range(RING)]


def block_moves(back):
    moves = []
    for outer in range(OUTERS):
        for member in range(MEMBERS):
            owner = member * OUTERS + outer
            here = outer * MEMBERS + member
            moves.append((here, owner) if back else (owner, here))
    return moves


def spread_columns(block, parts):
    rows = block.shape[0]
    return block.reshape(rows, parts, MEMBERS, -1).transpose(2, 0, 1, 3).reshape(MEMBERS, rows, -1)


def join_columns(pieces, parts):
    members, rows, width = pieces.shape
    turned = pieces.reshape(members, rows, parts, width // parts).transpose(1, 2, 0, 3)
    return turned.reshape(rows, members * width)


def local(
    tokens,
    cotangent,
    attn_weight,
    mlp_weight,
    small_weight,
    attn_first,
    attn_second,
    mlp_first,
    mlp_second,
    small_first,
    small_second,
):
    length, width = tokens.shape
    own_rows = attn_weight.shape[0]
    slab = own_rows * MEMBERS
    hidden = mlp_weight.shape[1] // 3 // MEMBERS
    inner = width // MEMBERS
    heads = inner // HEAD
    member = lax.axis_index(GROUP)

    rows_all = lax.all_gather(jnp.concatenate([tokens, cotangent], axis=1), GROUP, axis=0, tiled=True)

    attn_low = attn_weight.astype(LOW)
    small_low = jnp.pad(small_weight.astype(LOW).T, ((0, 0), (0, 121)))
    columns = 3 * inner + 128
    sent = jnp.concatenate(
        [
            spread_columns(attn_low[:, : 3 * width], 3),
            jnp.broadcast_to(small_low, (MEMBERS, own_rows, 128)),
            spread_columns(mlp_weight.astype(LOW), 3),
        ],
        axis=2,
    )
    slabs = lax.all_to_all(sent, GROUP, 0, 0, tiled=True).reshape(slab, columns + 3 * hidden)
    out_block = lax.ppermute(attn_low[:, 3 * width :], EVERY, block_moves(False))
    out_block = out_block.reshape(own_rows, MEMBERS, inner).transpose(1, 0, 2).reshape(slab, inner)
    mlp_part = lax.all_gather(slabs[:, columns:], OUTER, axis=0, tiled=True)
    places = group_places()
    tokens_all = [blocks_at(rows_all, part, length, 0) for part in places]
    attn_part = gather_outer(jnp.concatenate([slabs[:, :columns], out_block], axis=1))
    params = attn_part[:, 3 * inner : 3 * inner + 7].T.astype(FULL)
    bias = lax.dynamic_slice_in_dim(params[4:7], member * inner, inner, axis=1).reshape(1, -1)
    weight_wide = mlp_part[:, : 2 * hidden]
    weight_down = mlp_part[:, 2 * hidden :]

    tables = rope_tables(length, length, inner)
    cotangent_all = [jnp.concatenate(blocks_at(rows_all, part, length, width), axis=0) for part in places]

    def forward(blocks):
        return attend(blocks, attn_part, params[:2], bias, tables)

    ring = Scatter()
    kept = {2: forward(tokens_all[2])}
    ring.far(kept[2][3:])
    near_in = hold(tokens_all[1], ring.sum)
    ring.first()
    kept[1] = forward(near_in)
    ring.near(hold(kept[1][3:], ring.arrived))
    own_in, cotangent_all = hold((tokens_all[0], cotangent_all), ring.merge())
    own_in = hold(own_in, cotangent_all)
    ring.second()
    kept[0] = forward(own_in)
    ring.arrived = hold(ring.arrived, kept[0][3:])
    residual, normed_two = by_rows(
        residual_kernel,
        length,
        (tokens, kept[0][3], ring.arrived, sibling(add(kept[0][4], ring.arrived[length:]).astype(LOW))),
        params,
        (((length, width), FULL), ((length, width), LOW)),
        "residual",
    )
    normed_low, turned, mixed_low = ([kept[p][i] for p in range(3)] for i in range(3))

    def feed(part, blocks):
        rows = jnp.concatenate(blocks, axis=0)
        both = product(rows, weight_wide, ((1,), (0,)))
        gate, upward = (both[:, :hidden], both[:, hidden:])
        sigma = jax.nn.sigmoid(gate)
        active = gate * sigma
        hidden_low = (active * upward).astype(LOW)
        back_hidden = product(cotangent_all[part], weight_down, ((1,), (0,)))
        back_gate = (back_hidden * upward * sigma * (1.0 + gate * (1.0 - sigma))).astype(LOW)
        back_wide = jnp.concatenate([back_gate, (back_hidden * active).astype(LOW)], axis=1)
        share = product(back_wide, weight_wide, ((1,), (1,))).astype(LOW)
        return (rows, hidden_low, back_wide, share)

    def halves_of(rows):
        half = rows.shape[0] // 2
        return (rows[:half], rows[half:])

    def out_share(part):
        return product(hidden_low[part], weight_down, ((1,), (1,))).astype(LOW)

    _, done = gather_group(normed_two, feed)
    normed_two, hidden_low, back_wide, shares = (list(made) for made in zip(*done))
    ring = Scatter()
    ring.near(halves_of(shares[1]))
    ring.far(halves_of(shares[2]))
    hidden_low = hold(hidden_low, ring.sum)
    ring.first()
    out_shares = [out_share(part) for part in range(3)]
    ring.arrived = hold(ring.arrived, out_shares)
    ring.merge()
    back_wide = hold(back_wide, ring.sum)
    ring.second()
    mlp_grad = weight_grad([(normed_two, back_wide), (cotangent_all, hidden_low)], 512, 36)
    ring.arrived = hold(ring.arrived, mlp_grad)
    back_residual, back_low, norm_two_grads = by_rows(
        functools.partial(norm_back_kernel, 3, 2, True),
        length,
        (residual, cotangent, *ring.own(shares[0])),
        params,
        (((length, width), FULL), ((length, width), LOW), ((16, width), FULL)),
        "norm_back",
    )
    mlp_grad = lax.psum_scatter(mlp_grad, OUTER, scatter_dimension=0, tiled=True)

    back_sums = [jnp.zeros((8, 3 * inner), FULL), jnp.zeros((16, width), FULL), jnp.zeros((MEMBERS * length, width), LOW)]
    ring = Scatter()
    taken, out_grads = ([], [])

    def out_grad():
        grad = weight_grad([(mixed_low, taken)], inner, 16)
        grad = grad.reshape(OUTERS, own_rows, MEMBERS, inner).transpose(0, 2, 1, 3)
        return grad.reshape(width, inner)

    def backward(part, blocks):
        if part == 1:
            ring.far(hold(halves_of(out_shares[2]), blocks[0]))
            blocks = hold(blocks, ring.sum)
            ring.first()
        elif part == 2:
            blocks = hold(blocks, ring.merge())
            ring.second()
        taken.extend(blocks)
        if part == 2:
            out_grads[:] = [out_grad()]
            blocks = hold(blocks, out_grads)
        made = attend_back(
            places[part], blocks, tokens_all[part], attn_part, turned[part], *back_sums, tables, (10, 50, 25)[part]
        )
        back_sums[:] = made[1:]
        if part == 0:
            return (made[0], (made[1], ring.near(halves_of(out_shares[1]))))
        return made[:2]

    _, done = gather_group(back_low, backward)
    back_proj = [made[0] for made in done]

    bias_rows = jnp.pad(
        back_sums[0][0].reshape(3, OUTERS, own_rows), ((0, 5), (0, 0), (0, slab - own_rows))
    ).reshape(8, width)
    back_proj = hold(back_proj, ring.arrived)
    halves = attn_grads(normed_low, back_proj, back_sums[1], norm_two_grads, bias_rows, out_grads[0])
    output = add(residual, *(rows[:length] for rows in ring.own(hold(out_shares[0], halves))))
    parts = [[half[j] for j in range(RING)] for half in halves]
    arrived = [far_step(part[2], axis) for part, axis in zip(parts, OUTER)]
    shares = [near_shares(part[1], part[3], halves) for part, halves in zip(parts, arrived)]
    totals = [
        add(part[0], *near_step(share, axis)).astype(LOW) for part, share, axis in zip(parts, shares, OUTER)
    ]
    back_normed_one = lax.psum_scatter(hold(back_sums[2], shares), GROUP, scatter_dimension=0, tiled=True)
    fill = jnp.zeros((slab, columns), LOW)
    blank = jnp.zeros((slab, -(columns + 3 * hidden) % 128), LOW)
    pieces = jnp.concatenate([fill, mlp_grad, blank], axis=1)
    totals = hold(totals, pieces, output)
    totals = [
        reduce_ring([total[j] for j in range(RING)], axis).astype(LOW) for total, axis in zip(totals, OUTER[::-1])
    ]
    attn_grad = hold(jnp.concatenate(totals, axis=0), back_normed_one)
    (grad_tokens,) = by_rows(
        functools.partial(norm_back_kernel, 1, 0, False),
        length,
        (tokens, back_residual, back_normed_one),
        params,
        (((length, width), FULL),),
        "norm_back",
    )
    out_grad = (
        attn_grad[:, 3 * inner + 128 :]
        .reshape(MEMBERS, own_rows, inner)
        .transpose(1, 0, 2)
        .reshape(own_rows, width)
    )
    bias_grad = attn_grad[:own_rows, 3 * inner : 3 * inner + 128]
    block = lax.ppermute(
        jnp.concatenate([out_grad, bias_grad], axis=1), EVERY, block_moves(True)
    ).astype(FULL)
    pieces = lax.dynamic_update_slice(pieces, attn_grad[:, :columns], (0, 0)).reshape(MEMBERS, own_rows, -1)
    all_pieces = lax.all_to_all(pieces, GROUP, 0, 0, tiled=True)
    pieces = all_pieces[:, :, :columns].astype(FULL)
    attn_grad = jnp.concatenate(
        [join_columns(pieces[:, :, : 3 * inner], 3), block[:, :width]], axis=1
    )
    norm_grads = jnp.sum(pieces[:, :, 3 * inner : 3 * inner + 4], axis=0)
    small_grad = jnp.concatenate([norm_grads, block[:, width + 4 : width + 7]], axis=1).T

    attn_new, attn_first_new, attn_second_new = adamw(
        attn_weight, attn_grad, attn_first, attn_second, rate_matrix, decay_matrix
    )
    mlp_new, mlp_first_new, mlp_second_new = adamw_mlp(all_pieces, columns, mlp_weight, mlp_first, mlp_second)
    small_new, small_first_new, small_second_new = adamw(
        small_weight, small_grad, small_first, small_second, rate_small, 0.0
    )
    return (
        output.astype(LOW),
        grad_tokens,
        attn_new,
        attn_first_new,
        attn_second_new,
        mlp_new,
        mlp_first_new,
        mlp_second_new,
        small_new,
        small_first_new,
        small_second_new,
    )


def solution(mesh):
    grid = Mesh(mesh.devices.reshape(4, 4, 4, 2), EVERY)
    rows, columns = (P(EVERY, None), P(None, EVERY))
    return jax.shard_map(
        local,
        mesh=grid,
        in_specs=(rows,) * 4 + (columns,) + (rows,) * 4 + (columns,) * 2,
        out_specs=(rows,) * 8 + (columns,) * 3,
        check_vma=False,
    )
```

```python
import functools

import jax
import jax.numpy as jnp
from jax import lax
from jax.experimental import pallas as pl
from jax.experimental.pallas import tpu as pltpu
from jax.sharding import Mesh, PartitionSpec as P

HEAD = 64
ROT = 16
STEP = 10

norm_eps = 1e-05
mask_fill = -1000000000.0
rope_base = 10000.0
beta_one = 0.9
beta_two = 0.95
adam_eps = 1e-08
rate_matrix = 0.01
rate_small = 0.1
decay_matrix = 0.1

LOW = jnp.bfloat16
FULL = jnp.float32

OUTER = ("y", "z")
GROUP = ("x", "core")
EVERY = OUTER + GROUP
RING = 4
MEMBERS = 8
OUTERS = 16


def product(left, right, dims):
    return lax.dot_general(left, right, (dims, ((), ())), preferred_element_type=FULL)


def normalize(values):
    center = values - jnp.mean(values, axis=-1, keepdims=True)
    spread = jnp.mean(center * center, axis=-1, keepdims=True)
    scaled = lax.rsqrt(spread + norm_eps)
    return (center * scaled, scaled)


def norm_back(grad_normed, normal, scaled, gain):
    grad_hat = grad_normed * gain
    return scaled * (
        grad_hat
        - jnp.mean(grad_hat, axis=-1, keepdims=True)
        - normal * jnp.mean(grad_hat * normal, axis=-1, keepdims=True)
    )


def rope_tables(rows, length, inner):
    half = ROT // 2
    lane = jnp.arange(inner) % HEAD
    position = (jnp.arange(rows) % length).astype(FULL)
    inverse = rope_base ** (-((lane % half).astype(FULL) * 2.0 / ROT))
    angle = position[:, None] * inverse[None, :]
    cosine = jnp.where(lane < ROT, jnp.cos(angle), 1.0)
    later = jnp.where(lane < half, -jnp.sin(angle), 0.0)
    earlier = jnp.where((lane >= half) & (lane < ROT), jnp.sin(angle), 0.0)
    return (cosine, later, earlier)


def rotate(values, tables, sign):
    cosine, later, earlier = tables
    half, lanes = (ROT // 2, values.shape[1])
    moved = pltpu.roll(values, lanes - half, 1) * later[...] + pltpu.roll(values, half, 1) * earlier[...]
    return values * cosine[...] + sign * moved


def pair_masks(length):
    rows = lax.broadcasted_iota(jnp.int32, (length, length), 0)
    columns = lax.broadcasted_iota(jnp.int32, (length, length), 1)
    lanes = lax.broadcasted_iota(jnp.int32, (length, 2 * HEAD), 1)
    return (rows >= columns, lanes < HEAD)


def score(query, keyed, causal):
    return jnp.where(causal, product(query, keyed, ((1,), (1,))), mask_fill)


def soft(scores):
    top = jnp.max(scores, axis=-1, keepdims=True)
    weights = jnp.exp(scores - top)
    total = jnp.sum(weights, axis=-1, keepdims=True)
    return (weights / total, top + jnp.log(total))


def out_columns(weights, inner, piece):
    start, step = (weights.shape[1] - inner, weights.shape[0] // OUTERS)
    rows = step // MEMBERS
    return jnp.concatenate(
        [weights[k * step + piece * rows : k * step + (piece + 1) * rows, start:] for k in range(OUTERS)], axis=0
    )


def attend_kernel(count, *refs):
    tokens, (weights, norm, bias, *tables) = (refs[:count], refs[count : count + 6])
    normed, turned, mixed, logs, *branches = refs[count + 6 :]
    length, inner = (tokens[0].shape[0], bias.shape[1] // 3)
    causal, first = pair_masks(length)
    for block, part in enumerate(tokens):
        rows = slice(block * length, (block + 1) * length)
        normal, _ = normalize(part[...].astype(FULL))
        normed[rows] = (normal * norm[0:1] + norm[1:2]).astype(LOW)
    projected = product(normed[...], weights[:, : 3 * inner], ((1,), (0,))) + bias[...]
    for block in range(count):
        rows = slice(block * length, (block + 1) * length)
        query = rotate(projected[rows, :inner], tables, 1.0).astype(LOW)
        keyed = rotate(projected[rows, inner : 2 * inner], tables, 1.0).astype(LOW)
        valued = projected[rows, 2 * inner :].astype(LOW)
        turned[rows, :inner] = query
        turned[rows, inner : 2 * inner] = keyed
        turned[rows, 2 * inner :] = valued
        for column in range(0, inner, 2 * HEAD):
            at = slice(column, column + 2 * HEAD)
            outs = []
            for head, side in enumerate((first, ~first), column // HEAD):
                query_one = jnp.where(side, query[:, at] * HEAD**-0.5, 0)
                prob, log = soft(score(query_one, keyed[:, at], causal))
                logs[rows, head : head + 1] = log
                outs.append(product(prob.astype(LOW), valued[:, at], ((1,), (0,))))
            mixed[rows, at] = jnp.where(first, outs[0], outs[1]).astype(LOW)
    half = length * count // 2
    for piece in range(MEMBERS):
        share = product(mixed[...], out_columns(weights, inner, piece), ((1,), (0,))).astype(LOW)
        for at, branch in enumerate(branches):
            branch[:, piece * inner : (piece + 1) * inner] = share[at * half : (at + 1) * half]


def attend(blocks, weights, norm, bias, tables):
    length, width = blocks[0].shape
    rows, inner = (length * len(blocks), bias.shape[1] // 3)
    shapes = [jax.ShapeDtypeStruct((rows, n), LOW) for n in (width, 3 * inner, inner)]
    shapes += [jax.ShapeDtypeStruct((rows, 128), FULL)] + [jax.ShapeDtypeStruct((rows // 2, width), LOW)] * 2
    return pl.pallas_call(
        functools.partial(attend_kernel, len(blocks)),
        out_shape=shapes,
        compiler_params=pltpu.CompilerParams(vmem_limit_bytes=28 << 20),
        cost_estimate=pl.CostEstimate(flops=10**9, bytes_accessed=rows * width, transcendentals=0),
        name="attend",
    )(*blocks, weights, norm, bias, *tables)


def attend_back_kernel(count, places, *refs):
    grads, tokens, refs = (refs[:count], refs[count : 2 * count], refs[2 * count :])
    weights, turned, logs, sums_in, norm_in, *tables = refs[:8]
    back, sums, norm_sums, shares, back_mixed, normed_grad, low_grad, sent = refs[9:]
    length, inner = (grads[0].shape[0], turned.shape[1] // 3)
    total = 0.0
    for piece in range(MEMBERS):
        columns = slice(piece * inner, (piece + 1) * inner)
        rows = jnp.concatenate([grad[:, columns] for grad in grads], axis=0)
        total += product(rows, out_columns(weights, inner, piece), ((1,), (1,)))
    back_mixed[...] = total.astype(LOW)
    causal, first = pair_masks(length)
    bias_total = sums_in[...]
    for block in range(count):
        rows = slice(block * length, (block + 1) * length)
        parts = []
        for column in range(0, inner, 2 * HEAD):
            query, keyed, valued = (
                turned[rows, part * inner + column : part * inner + column + 2 * HEAD] for part in range(3)
            )
            grad_pair = back_mixed[rows, column : column + 2 * HEAD]
            back_query, back_key, back_value = ([], 0.0, 0.0)
            for head, side in enumerate((first, ~first), column // HEAD):
                query_one = jnp.where(side, query * HEAD**-0.5, 0)
                grad_one = jnp.where(side, grad_pair, 0)
                prob = jnp.exp(score(query_one, keyed, causal) - logs[rows, head : head + 1])
                back_value += product(prob.astype(LOW), grad_one, ((0,), (0,)))
                grad_prob = product(grad_one, valued, ((1,), (1,)))
                delta = jnp.sum(prob * grad_prob, axis=-1, keepdims=True)
                grad_scores = (prob * (grad_prob - delta)).astype(LOW)
                back_query.append(product(grad_scores, keyed, ((1,), (0,))))
                back_key += product(grad_scores, query_one, ((0,), (0,)))
            back_query = jnp.where(first, back_query[0], back_query[1]) * HEAD**-0.5
            parts.append((back_query, back_key, back_value))
        back_query, back_key, back_value = (jnp.concatenate(side, axis=1) for side in zip(*parts))
        back[rows, :inner] = rotate(back_query, tables, -1.0).astype(LOW)
        back[rows, inner : 2 * inner] = rotate(back_key, tables, -1.0).astype(LOW)
        back[rows, 2 * inner :] = back_value.astype(LOW)
        bias_total += jnp.sum(back[rows].astype(FULL), axis=0, keepdims=True)
    sums[...] = bias_total
    normed_grad[...] = product(back[...], weights[:, : 3 * inner], ((1,), (1,)))
    scale_total, shift_total = (norm_in[0:8], norm_in[8:16])
    leaving = []
    for block in range(count):
        rows = slice(block * length, (block + 1) * length)
        low_grad[rows] = normed_grad[rows].astype(LOW)
        there = pl.ds(pl.multiple_of(places[block] * length, length), length)
        leaving.append(pltpu.make_async_copy(low_grad.at[rows], shares.at[there], sent.at[block]))
        leaving[-1].start()
    for block in range(count):
        rows = slice(block * length, (block + 1) * length)
        grad = normed_grad[rows]
        normal, _ = normalize(tokens[block][...].astype(FULL))
        scale_total += jnp.sum(grad * normal, axis=0, keepdims=True)
        shift_total += jnp.sum(grad, axis=0, keepdims=True)
    norm_sums[0:8] = scale_total
    norm_sums[8:16] = shift_total
    for copy in leaving:
        copy.wait()


def attend_back(places, grads, tokens, weights, turned, logs, sums, norm_sums, shares, tables, micros):
    length, width = grads[0].shape
    count, (rows, columns) = (len(grads), turned.shape)
    made = (jax.ShapeDtypeStruct((rows, columns), LOW), sums, norm_sums, shares)
    operands = (places, *grads, *tokens, weights, turned, logs, sums, norm_sums, *tables, shares)
    vmem, away = (pl.BlockSpec(memory_space=pltpu.VMEM), pl.BlockSpec(memory_space=pltpu.HBM))
    return pl.pallas_call(
        functools.partial(attend_back_kernel, count),
        in_specs=[pl.BlockSpec(memory_space=pltpu.SMEM)] + [vmem] * (len(operands) - 2) + [away],
        out_specs=[vmem] * 3 + [away],
        out_shape=[jax.ShapeDtypeStruct(m.shape, m.dtype) for m in made],
        scratch_shapes=[
            pltpu.VMEM((rows, columns // 3), LOW),
            pltpu.VMEM((rows, width), FULL),
            pltpu.VMEM((rows, width), LOW),
            pltpu.SemaphoreType.DMA((count,)),
        ],
        input_output_aliases={len(operands) - 1: 3},
        compiler_params=pltpu.CompilerParams(vmem_limit_bytes=28 << 20),
        cost_estimate=pl.CostEstimate(flops=micros * 10**9, bytes_accessed=rows * width, transcendentals=0),
        name="attend_back",
    )(*operands)


def residual_kernel(tokens, mine, arrived, twin, norm, residual, normed):
    total = tokens[...].astype(FULL) + mine[...].astype(FULL) + arrived[...].astype(FULL) + twin[...].astype(FULL)
    residual[...] = total
    normal, _ = normalize(total)
    normed[...] = (normal * norm[2:3] + norm[3:4]).astype(LOW)


def norm_back_kernel(given, row, low, values, base, *refs):
    grad = sum(g[...].astype(FULL) for g in refs[:given])
    norm, outs = (refs[given], refs[given + 1 :])
    normal, scaled = normalize(values[...].astype(FULL))
    total = base[...].astype(FULL) + norm_back(grad, normal, scaled, norm[row : row + 1])
    outs[0][...] = total
    if low:
        outs[1][...] = total.astype(LOW)

        @pl.when(pl.program_id(0) == 0)
        def _():
            outs[2][...] = jnp.zeros_like(outs[2])

        outs[2][0:8] += jnp.broadcast_to(jnp.sum(grad * normal, axis=0, keepdims=True), (8, grad.shape[1]))
        outs[2][8:16] += jnp.broadcast_to(jnp.sum(grad, axis=0, keepdims=True), (8, grad.shape[1]))


def by_rows(kernel, rows, operands, norm, shapes, name):
    block = rows // 2
    width = operands[0].shape[1]
    spot = pl.BlockSpec((block, width), lambda i: (i, 0))
    whole = [pl.BlockSpec(norm.shape, lambda i: (0, 0))] if norm is not None else []
    return pl.pallas_call(
        kernel,
        grid=(rows // block,),
        in_specs=[spot] * len(operands) + whole,
        out_specs=[spot if shape[0] == rows else pl.BlockSpec(shape, lambda i: (0, 0)) for shape, _ in shapes],
        out_shape=[jax.ShapeDtypeStruct(shape, kind) for shape, kind in shapes],
        compiler_params=pltpu.CompilerParams(vmem_limit_bytes=16 << 20),
        cost_estimate=pl.CostEstimate(flops=10**8, bytes_accessed=10**6, transcendentals=0),
        name=name,
    )(*operands, *([norm] if whole else []))


def join_kernel(first, second, both):
    rows = first.shape[0]
    both[:rows] = first[...]
    both[rows:] = second[...]


def join_rows(first, second):
    rows, width = first.shape
    return pl.pallas_call(
        join_kernel,
        out_shape=jax.ShapeDtypeStruct((2 * rows, width), first.dtype),
        compiler_params=pltpu.CompilerParams(vmem_limit_bytes=8 << 20),
        cost_estimate=pl.CostEstimate(flops=1, bytes_accessed=1, transcendentals=0),
        name="join_rows",
    )(first, second)


def weight_grad_kernel(sizes, *refs):
    out, at, column = (refs[-1], 0, 0)
    for count in sizes:
        if count:
            lefts, rights = (refs[at : at + count[0]], refs[at + count[0] : at + sum(count)])
            total, rights = (0.0, list(rights))
            for left in lefts:
                right = [rights.pop(0)[...]]
                while sum(r.shape[0] for r in right) < left.shape[0]:
                    right.append(rights.pop(0)[...])
                total += product(left[...], jnp.concatenate(right, axis=0), ((0,), (0,)))
            at += sum(count)
        else:
            total = refs[at][...]
            if total.shape[0] == 8:
                total = jnp.concatenate([total, jnp.zeros((120, total.shape[1]), FULL)], axis=0).T
            at += 1
        out[:, column : column + total.shape[1]] = total.astype(LOW)
        column += total.shape[1]


def weight_grad(terms, block, limit):
    sizes, operands, specs, wide = ([], [], [], 0)
    for term in terms:
        if isinstance(term, tuple):
            lefts, rights = term
            height = lefts[0].shape[1]
            rows = min(block, height)
            columns = rights[0].shape[1]
            sizes.append((len(lefts), len(rights)))
            operands += [*lefts, *rights]
            specs += [pl.BlockSpec((left.shape[0], rows), lambda i: (0, i)) for left in lefts]
            specs += [pl.BlockSpec(right.shape, lambda i: (0, 0)) for right in rights]
        elif term.shape[0] == 8:
            columns = 128
            sizes.append(())
            operands.append(term)
            specs.append(pl.BlockSpec((8, rows), lambda i: (0, i)))
        else:
            columns = term.shape[1]
            sizes.append(())
            operands.append(term)
            specs.append(pl.BlockSpec((rows, columns), lambda i: (i, 0)))
        wide += columns
    return pl.pallas_call(
        functools.partial(weight_grad_kernel, tuple(sizes)),
        grid=(height // rows,),
        in_specs=specs,
        out_specs=pl.BlockSpec((rows, wide), lambda i: (i, 0)),
        out_shape=jax.ShapeDtypeStruct((height, wide), LOW),
        compiler_params=pltpu.CompilerParams(vmem_limit_bytes=limit << 20),
        cost_estimate=pl.CostEstimate(flops=height * wide, bytes_accessed=height * wide, transcendentals=0),
        name="weight_grad",
    )(*operands)


def attn_grad_kernel(count, place, *refs):
    lefts, rights = (refs[:count], refs[count : 2 * count])
    one, two, bias, packed, first, second = refs[2 * count :]
    grad = 0.0
    for left, right in zip(lefts, rights):
        grad += product(left[...], right[...], ((0,), (0,)))
    columns, rows = (grad.shape[1], grad.shape[0] // RING)
    small = jnp.concatenate([one[0:1], one[8:9], two[0:1], two[8:9], bias[0:4]], axis=0)
    small = jnp.concatenate([small, jnp.zeros((120, small.shape[1]), FULL)], axis=0).T
    for z in range(RING):
        spot = lax.rem(z + RING - place[1], RING)
        for half, (out, at) in enumerate(((first, (0, spot)), (second, (spot, 0)))):
            here = slice(z * rows + half * rows // 2, z * rows + (half + 1) * rows // 2)
            out[(*at, slice(None), slice(0, columns))] = grad[here].astype(LOW)
            out[(*at, slice(None), slice(columns, columns + 128))] = small[here].astype(LOW)
            out[(*at, slice(None), slice(columns + 128, None))] = packed[here]


def attn_grads(lefts, rights, norm_one, norm_two, bias, packed):
    width, columns = (lefts[0].shape[1], rights[0].shape[1])
    wide, rows = (columns + 128 + packed.shape[1], width // RING)
    place = jnp.stack([lax.axis_index(axis) for axis in OUTER]).astype(jnp.int32)
    half = rows // RING // 2

    def here(j, place):
        return lax.rem(place[0] + j, RING)

    return pl.pallas_call(
        functools.partial(attn_grad_kernel, len(lefts)),
        grid_spec=pltpu.PrefetchScalarGridSpec(
            num_scalar_prefetch=1,
            grid=(RING,),
            in_specs=[pl.BlockSpec((left.shape[0], rows), lambda j, place: (0, here(j, place))) for left in lefts]
            + [pl.BlockSpec(right.shape, lambda j, place: (0, 0)) for right in rights]
            + [pl.BlockSpec((a.shape[0], rows), lambda j, place: (0, here(j, place))) for a in (norm_one, norm_two, bias)]
            + [pl.BlockSpec((rows, packed.shape[1]), lambda j, place: (here(j, place), 0))],
            out_specs=[
                pl.BlockSpec((1, RING, half, wide), lambda j, place: (j, 0, 0, 0)),
                pl.BlockSpec((RING, 1, half, wide), lambda j, place: (0, j, 0, 0)),
            ],
        ),
        out_shape=[jax.ShapeDtypeStruct((RING, RING, half, wide), LOW)] * 2,
        compiler_params=pltpu.CompilerParams(vmem_limit_bytes=60 << 20),
        cost_estimate=pl.CostEstimate(flops=10**9, bytes_accessed=10**6, transcendentals=0),
        name="attn_grads",
    )(place, *lefts, *rights, norm_one, norm_two, bias, packed)


def out_grad_kernel(count, *refs):
    mixed, grads, packed = (refs[:count], list(refs[count:-1]), refs[-1])
    total = 0.0
    for left in mixed:
        right = []
        while sum(r.shape[0] for r in right) < left.shape[0]:
            right.append(grads.pop(0)[...])
        total += product(left[...], jnp.concatenate(right, axis=0), ((0,), (0,)))
    total = total.astype(LOW)
    step, inner = (packed.shape[0] // OUTERS, packed.shape[1])
    rows = step // MEMBERS
    for outer in range(OUTERS):
        for piece in range(MEMBERS):
            start = outer * step + piece * rows
            packed[start : start + rows] = total[outer * rows : (outer + 1) * rows, piece * inner : (piece + 1) * inner]


def packed_out_grad(mixed, grads):
    width, inner = (grads[0].shape[1], mixed[0].shape[1])
    return pl.pallas_call(
        functools.partial(out_grad_kernel, len(mixed)),
        out_shape=jax.ShapeDtypeStruct((width, inner), LOW),
        compiler_params=pltpu.CompilerParams(vmem_limit_bytes=16 << 20),
        cost_estimate=pl.CostEstimate(flops=width * inner, bytes_accessed=width * inner, transcendentals=0),
        name="out_grad",
    )(*mixed, *grads)


def adamw(weight, grad, first, second, rate, decay):
    first_new = beta_one * first + (1.0 - beta_one) * grad
    second_new = beta_two * second + (1.0 - beta_two) * grad * grad
    corr_one = 1.0 - beta_one**STEP
    corr_two = 1.0 - beta_two**STEP
    update = first_new / corr_one / (jnp.sqrt(second_new / corr_two) + adam_eps)
    return (weight - rate * (update + decay * weight), first_new, second_new)


def adamw_kernel(skip, pieces, weight, first, second, *outs):
    rows, wide = (weight.shape[0], weight.shape[1] // (pieces.shape[0] // 2))
    half = wide // 2
    across = -(-half // 128) * 128
    lanes = lax.broadcasted_iota(jnp.int32, (rows, wide), 1)
    blank = jnp.zeros((rows, wide - across), FULL)

    def turned(member, start, target):
        base = start // 128 * 128
        values = pieces[member, :, base : base + across].astype(FULL)
        move = (target - (start - base)) % across
        return pltpu.roll(values, move, 1) if move else values

    for part in range(3):

        @pl.when(pl.program_id(0) == part)
        def _():
            start = skip + part * half
            for pair in range(pieces.shape[0] // 2):
                left = jnp.concatenate([turned(2 * pair, start, 0), blank], axis=1)
                right = jnp.concatenate([blank, turned(2 * pair + 1, start, across - half)], axis=1)
                grad = jnp.where(lanes < half, left, right)
                at = (slice(None), slice(pair * wide, (pair + 1) * wide))
                made = adamw(weight[at], grad, first[at], second[at], rate_matrix, decay_matrix)
                for out, value in zip(outs, made):
                    out[at] = value


def adamw_mlp(pieces, skip, weight, first, second):
    rows, width = weight.shape
    spot = pl.BlockSpec((rows, width // 3), lambda part: (0, part))
    return pl.pallas_call(
        functools.partial(adamw_kernel, skip),
        grid=(3,),
        in_specs=[pl.BlockSpec(pieces.shape, lambda part: (0, 0, 0))] + [spot] * 3,
        out_specs=[spot] * 3,
        out_shape=[jax.ShapeDtypeStruct(weight.shape, FULL)] * 3,
        compiler_params=pltpu.CompilerParams(vmem_limit_bytes=24 << 20),
        cost_estimate=pl.CostEstimate(flops=10**8, bytes_accessed=7 * 4 * weight.size, transcendentals=0),
        name="adamw",
    )(pieces, weight, first, second)


def shift(values, axis, hop):
    return lax.ppermute(values, axis, [(i, (i + hop) % RING) for i in range(RING)])


def sibling(values):
    return lax.ppermute(values, "core", [(0, 1), (1, 0)])


def add(*values):
    return sum(v.astype(FULL) for v in values)


def hold(values, *others):
    return lax.optimization_barrier((values, others))[0]


def blocks_at(rows, places, length, column):
    width = rows.shape[1] // 2
    return [lax.dynamic_slice(rows, (place * length, column), (length, width)) for place in places]


def onward(values, back=False):
    moves = []
    for chip in range(RING):
        for core, hop in ((0, 1), (1, -1)):
            moves.append((2 * chip + core, 2 * ((chip + (-hop if back else hop)) % RING) + core))
    return lax.ppermute(values, GROUP, moves)


def group_places():
    chip, core = (lax.axis_index(axis) for axis in GROUP)
    one, two, far = ((chip + 3 + 2 * core) % RING, (chip + 1 + 2 * core) % RING, (chip + 2) % RING)
    other = 1 - core
    parts = (
        [2 * chip + core, 2 * chip + other],
        [2 * one + core, 2 * one + other, 2 * two + other, 2 * two + core],
        [2 * far + core, 2 * far + other],
    )
    return [jnp.stack(part).astype(jnp.int32) for part in parts]


def gather_group(values, work):
    rows = values.shape[0]
    own = join_rows(values, sibling(values))
    one = onward(own)
    parts = [[own[:rows], own[rows:]]]
    done = [work(0, parts[0])]
    one = hold(one, done[0][-1])
    far = onward(one[:rows])
    two = sibling(one)
    parts.append([one[:rows], one[rows:], two[:rows], two[rows:]])
    done.append(work(1, parts[1]))
    far = hold(far, done[1][-1])
    parts.append([far, sibling(far)])
    done.append(work(2, parts[2]))
    return (parts, done)


class Scatter:
    def far(self, blocks):
        self.sum = add(blocks[0], sibling(blocks[1])).astype(LOW)
        return self.sum

    def first(self):
        self.arrived = onward(self.sum, back=True)
        return self.arrived

    def near(self, blocks):
        self.both = add(blocks[0], sibling(blocks[1]))
        self.rows = self.both.shape[0] // 2
        return self.both

    def merge(self):
        rows = self.rows
        self.sum = jnp.concatenate([add(self.both[:rows], self.arrived), self.both[rows:]], axis=0).astype(LOW)
        return self.sum

    def second(self):
        self.arrived = onward(self.sum, back=True)
        return self.arrived

    def own(self, whole):
        rows = self.rows
        twin = sibling(add(whole[rows:], self.arrived[rows:]).astype(LOW))
        return (whole, self.arrived, twin)


def gather_outer(values):
    rows, columns = values.shape
    half = rows // 2
    place = {axis: lax.axis_index(axis) for axis in OUTER}

    def ring(block, axis, straight=False):
        before = shift(block, axis, 1)
        after = shift(block, axis, -1)
        if straight:
            return zip((block, before, after, shift(block, axis, 2)), [(place[axis] + j) % RING for j in (0, 3, 1, 2)], (0,) * 4)
        quarter = block.shape[0] // 2
        far = (shift(before[:quarter], axis, 1), shift(after[quarter:], axis, -1))
        spots = [(place[axis] + j) % RING for j in (0, 3, 1, 2, 2)]
        return zip((block, before, after, *far), spots, (0, 0, 0, 0, quarter))

    lines = []
    for axis, block in (("z", values[:half]), ("y", values[half:])):
        line = jnp.zeros((RING, half, columns), values.dtype)
        for piece, spot, start in ring(block, axis, True):
            line = lax.dynamic_update_slice(line, piece[None], (spot, start, 0))
        lines.append(line)
    whole = jnp.zeros((RING, RING, 2, half, columns), values.dtype)
    rings = [list(ring(line, axis)) for line, axis in zip(lines, ("y", "z"))]
    for piece, spot, start in rings[0]:
        whole = lax.dynamic_update_slice(whole, piece[None, :, None], (spot, start, 0, 0, 0))
    for piece, spot, start in rings[1]:
        whole = lax.dynamic_update_slice(whole, piece[:, None, None], (start, spot, 1, 0, 0))
    return whole.reshape(OUTERS * rows, columns)


def far_step(far, axis):
    half = far.shape[0] // 2
    return (shift(far[:half], axis, 1), shift(far[half:], axis, -1))


def near_shares(next_part, last_part, arrived):
    up, down = arrived
    half = up.shape[0]
    after = lax.dynamic_update_slice_in_dim(next_part, add(next_part[:half], up).astype(LOW), 0, 0)
    before = lax.dynamic_update_slice_in_dim(last_part, add(last_part[half:], down).astype(LOW), half, 0)
    return (after, before)


def near_step(shares, axis):
    return (shift(shares[0], axis, 1), shift(shares[1], axis, -1))


def reduce_ring(parts, axis):
    return add(parts[0], *(shift(parts[j], axis, j) for j in (1, 3, 2)))


def ring_order(values, axis, dim):
    place = lax.axis_index(axis)
    return [lax.dynamic_index_in_dim(values, (place + j) % RING, dim, keepdims=False) for j in range(RING)]


def block_moves(back):
    moves = []
    for outer in range(OUTERS):
        for member in range(MEMBERS):
            owner = member * OUTERS + outer
            here = outer * MEMBERS + member
            moves.append((here, owner) if back else (owner, here))
    return moves


def spread_columns(block, parts):
    rows = block.shape[0]
    return block.reshape(rows, parts, MEMBERS, -1).transpose(2, 0, 1, 3).reshape(MEMBERS, rows, -1)


def join_columns(pieces, parts):
    members, rows, width = pieces.shape
    turned = pieces.reshape(members, rows, parts, width // parts).transpose(1, 2, 0, 3)
    return turned.reshape(rows, members * width)


def local(
    tokens,
    cotangent,
    attn_weight,
    mlp_weight,
    small_weight,
    attn_first,
    attn_second,
    mlp_first,
    mlp_second,
    small_first,
    small_second,
):
    length, width = tokens.shape
    own_rows = attn_weight.shape[0]
    slab = own_rows * MEMBERS
    hidden = mlp_weight.shape[1] // 3 // MEMBERS
    inner = width // MEMBERS
    heads = inner // HEAD
    member = lax.axis_index(GROUP)

    rows_all = lax.all_gather(jnp.concatenate([tokens, cotangent], axis=1), GROUP, axis=0, tiled=True)

    attn_low = attn_weight.astype(LOW)
    small_low = jnp.pad(small_weight.astype(LOW).T, ((0, 0), (0, 121)))
    columns = 3 * inner + 128
    sent = jnp.concatenate(
        [
            spread_columns(attn_low[:, : 3 * width], 3),
            jnp.broadcast_to(small_low, (MEMBERS, own_rows, 128)),
            spread_columns(mlp_weight.astype(LOW), 3),
        ],
        axis=2,
    )
    slabs = lax.all_to_all(sent, GROUP, 0, 0, tiled=True).reshape(slab, columns + 3 * hidden)
    out_block = lax.ppermute(attn_low[:, 3 * width :], EVERY, block_moves(False))
    out_block = out_block.reshape(own_rows, MEMBERS, inner).transpose(1, 0, 2).reshape(slab, inner)
    mlp_part = lax.all_gather(slabs[:, columns:], OUTER, axis=0, tiled=True)
    places = group_places()
    tokens_all = [blocks_at(rows_all, part, length, 0) for part in places]
    attn_part = gather_outer(jnp.concatenate([slabs[:, :columns], out_block], axis=1))
    params = attn_part[:, 3 * inner : 3 * inner + 7].T.astype(FULL)
    bias = lax.dynamic_slice_in_dim(params[4:7], member * inner, inner, axis=1).reshape(1, -1)
    weight_wide = mlp_part[:, : 2 * hidden]
    weight_down = mlp_part[:, 2 * hidden :]

    tables = rope_tables(length, length, inner)
    cotangent_all = [jnp.concatenate(blocks_at(rows_all, part, length, width), axis=0) for part in places]

    def forward(blocks):
        return attend(blocks, attn_part, params[:2], bias, tables)

    ring = Scatter()
    kept = {2: forward(tokens_all[2])}
    ring.far(kept[2][4:])
    near_in = hold(tokens_all[1], ring.sum)
    ring.first()
    kept[1] = forward(near_in)
    ring.near(hold(kept[1][4:], ring.arrived))
    own_in, cotangent_all = hold((tokens_all[0], cotangent_all), ring.merge())
    own_in = hold(own_in, cotangent_all)
    ring.second()
    kept[0] = forward(own_in)
    ring.arrived = hold(ring.arrived, kept[0][4:])
    residual, normed_two = by_rows(
        residual_kernel,
        length,
        (tokens, kept[0][4], ring.arrived, sibling(add(kept[0][5], ring.arrived[length:]).astype(LOW))),
        params,
        (((length, width), FULL), ((length, width), LOW)),
        "residual",
    )
    normed_low, turned, mixed_low, logs = ([kept[p][i] for p in range(3)] for i in range(4))

    def feed(part, blocks):
        rows = jnp.concatenate(blocks, axis=0)
        both = product(rows, weight_wide, ((1,), (0,)))
        gate, upward = (both[:, :hidden], both[:, hidden:])
        sigma = jax.nn.sigmoid(gate)
        active = gate * sigma
        hidden_low = (active * upward).astype(LOW)
        back_hidden = product(cotangent_all[part], weight_down, ((1,), (0,)))
        back_gate = (back_hidden * upward * sigma * (1.0 + gate * (1.0 - sigma))).astype(LOW)
        back_wide = jnp.concatenate([back_gate, (back_hidden * active).astype(LOW)], axis=1)
        share = product(back_wide, weight_wide, ((1,), (1,))).astype(LOW)
        return (rows, hidden_low, back_wide, share)

    def halves_of(rows):
        half = rows.shape[0] // 2
        return (rows[:half], rows[half:])

    def out_share(part):
        return product(hidden_low[part], weight_down, ((1,), (1,))).astype(LOW)

    _, done = gather_group(normed_two, feed)
    normed_two, hidden_low, back_wide, shares = (list(made) for made in zip(*done))
    ring = Scatter()
    ring.near(halves_of(shares[1]))
    ring.far(halves_of(shares[2]))
    back_wide = hold(back_wide, ring.sum)
    ring.first()
    mlp_grad = weight_grad([(normed_two, back_wide), (cotangent_all, hidden_low)], 512, 36)
    ring.arrived = hold(ring.arrived, mlp_grad)
    ring.merge()
    hidden_low = hold(hidden_low, ring.sum)
    ring.second()
    out_shares = [out_share(part) for part in range(3)]
    ring.arrived = hold(ring.arrived, out_shares)
    back_residual, back_low, norm_two_grads = by_rows(
        functools.partial(norm_back_kernel, 3, 2, True),
        length,
        (residual, cotangent, *ring.own(shares[0])),
        params,
        (((length, width), FULL), ((length, width), LOW), ((16, width), FULL)),
        "norm_back",
    )
    mlp_grad = lax.psum_scatter(mlp_grad, OUTER, scatter_dimension=0, tiled=True)

    back_sums = [jnp.zeros((8, 3 * inner), FULL), jnp.zeros((16, width), FULL), jnp.zeros((MEMBERS * length, width), LOW)]
    ring = Scatter()
    taken, out_grads = ([], [])

    def backward(part, blocks):
        if part == 1:
            ring.far(hold(halves_of(out_shares[2]), blocks[0]))
            blocks = hold(blocks, ring.sum)
            ring.first()
        elif part == 2:
            blocks = hold(blocks, ring.merge())
            ring.second()
        taken.extend(blocks)
        if part == 2:
            out_grads[:] = [packed_out_grad(mixed_low, taken)]
            blocks = hold(blocks, out_grads)
        made = attend_back(
            places[part], blocks, tokens_all[part], attn_part, turned[part], logs[part], *back_sums, tables, (20, 40, 20)[part]
        )
        back_sums[:] = made[1:]
        if part == 0:
            return (made[0], (made[1], ring.near(halves_of(out_shares[1]))))
        return made[:2]

    _, done = gather_group(back_low, backward)
    back_proj = [made[0] for made in done]

    bias_rows = jnp.pad(
        back_sums[0][0].reshape(3, OUTERS, own_rows), ((0, 5), (0, 0), (0, slab - own_rows))
    ).reshape(8, width)
    back_proj = hold(back_proj, ring.arrived)
    halves = attn_grads(normed_low, back_proj, back_sums[1], norm_two_grads, bias_rows, out_grads[0])
    output = add(residual, *(rows[:length] for rows in ring.own(hold(out_shares[0], halves))))
    parts = [[half[j] for j in range(RING)] for half in halves]
    arrived = [far_step(part[2], axis) for part, axis in zip(parts, OUTER)]
    shares = [near_shares(part[1], part[3], halves) for part, halves in zip(parts, arrived)]
    totals = [
        add(part[0], *near_step(share, axis)).astype(LOW) for part, share, axis in zip(parts, shares, OUTER)
    ]
    back_normed_one = lax.psum_scatter(hold(back_sums[2], shares), GROUP, scatter_dimension=0, tiled=True)
    fill = jnp.zeros((slab, columns), LOW)
    blank = jnp.zeros((slab, -(columns + 3 * hidden) % 128), LOW)
    pieces = jnp.concatenate([fill, mlp_grad, blank], axis=1)
    totals = hold(totals, pieces, output)
    totals = [
        reduce_ring([total[j] for j in range(RING)], axis).astype(LOW) for total, axis in zip(totals, OUTER[::-1])
    ]
    attn_grad = hold(jnp.concatenate(totals, axis=0), back_normed_one)
    (grad_tokens,) = by_rows(
        functools.partial(norm_back_kernel, 1, 0, False),
        length,
        (tokens, back_residual, back_normed_one),
        params,
        (((length, width), FULL),),
        "norm_back",
    )
    out_grad = (
        attn_grad[:, 3 * inner + 128 :]
        .reshape(MEMBERS, own_rows, inner)
        .transpose(1, 0, 2)
        .reshape(own_rows, width)
    )
    bias_grad = attn_grad[:own_rows, 3 * inner : 3 * inner + 128]
    block = lax.ppermute(
        jnp.concatenate([out_grad, bias_grad], axis=1), EVERY, block_moves(True)
    ).astype(FULL)
    pieces = lax.dynamic_update_slice(pieces, attn_grad[:, :columns], (0, 0)).reshape(MEMBERS, own_rows, -1)
    all_pieces = lax.all_to_all(pieces, GROUP, 0, 0, tiled=True)
    pieces = all_pieces[:, :, :columns].astype(FULL)
    attn_grad = jnp.concatenate(
        [join_columns(pieces[:, :, : 3 * inner], 3), block[:, :width]], axis=1
    )
    norm_grads = jnp.sum(pieces[:, :, 3 * inner : 3 * inner + 4], axis=0)
    small_grad = jnp.concatenate([norm_grads, block[:, width + 4 : width + 7]], axis=1).T

    attn_new, attn_first_new, attn_second_new = adamw(
        attn_weight, attn_grad, attn_first, attn_second, rate_matrix, decay_matrix
    )
    mlp_new, mlp_first_new, mlp_second_new = adamw_mlp(all_pieces, columns, mlp_weight, mlp_first, mlp_second)
    small_new, small_first_new, small_second_new = adamw(
        small_weight, small_grad, small_first, small_second, rate_small, 0.0
    )
    return (
        output.astype(LOW),
        grad_tokens,
        attn_new,
        attn_first_new,
        attn_second_new,
        mlp_new,
        mlp_first_new,
        mlp_second_new,
        small_new,
        small_first_new,
        small_second_new,
    )


def solution(mesh):
    grid = Mesh(mesh.devices.reshape(4, 4, 4, 2), EVERY)
    rows, columns = (P(EVERY, None), P(None, EVERY))
    return jax.shard_map(
        local,
        mesh=grid,
        in_specs=(rows,) * 4 + (columns,) + (rows,) * 4 + (columns,) * 2,
        out_specs=(rows,) * 8 + (columns,) * 3,
        check_vma=False,
    )
```

```python
import functools

import jax
import jax.numpy as jnp
from jax import lax
from jax.experimental import pallas as pl
from jax.experimental.pallas import tpu as pltpu
from jax.sharding import Mesh, PartitionSpec as P

HEAD = 64
ROT = 16
STEP = 10

norm_eps = 1e-05
mask_fill = -1000000000.0
rope_base = 10000.0
beta_one = 0.9
beta_two = 0.95
adam_eps = 1e-08
rate_matrix = 0.01
rate_small = 0.1
decay_matrix = 0.1

LOW = jnp.bfloat16
FULL = jnp.float32

OUTER = ("y", "z")
GROUP = ("x", "core")
EVERY = OUTER + GROUP
RING = 4
MEMBERS = 8
OUTERS = 16


def product(left, right, dims):
    return lax.dot_general(left, right, (dims, ((), ())), preferred_element_type=FULL)


def normalize(values):
    center = values - jnp.mean(values, axis=-1, keepdims=True)
    spread = jnp.mean(center * center, axis=-1, keepdims=True)
    scaled = lax.rsqrt(spread + norm_eps)
    return (center * scaled, scaled)


def norm_back(grad_normed, normal, scaled, gain):
    grad_hat = grad_normed * gain
    return scaled * (
        grad_hat
        - jnp.mean(grad_hat, axis=-1, keepdims=True)
        - normal * jnp.mean(grad_hat * normal, axis=-1, keepdims=True)
    )


def rope_tables(rows, length, inner):
    half = ROT // 2
    lane = jnp.arange(inner) % HEAD
    position = (jnp.arange(rows) % length).astype(FULL)
    inverse = rope_base ** (-((lane % half).astype(FULL) * 2.0 / ROT))
    angle = position[:, None] * inverse[None, :]
    cosine = jnp.where(lane < ROT, jnp.cos(angle), 1.0)
    later = jnp.where(lane < half, -jnp.sin(angle), 0.0)
    earlier = jnp.where((lane >= half) & (lane < ROT), jnp.sin(angle), 0.0)
    return (cosine, later, earlier)


def rotate(values, tables, sign):
    cosine, later, earlier = tables
    half, lanes = (ROT // 2, values.shape[1])
    moved = pltpu.roll(values, lanes - half, 1) * later[...] + pltpu.roll(values, half, 1) * earlier[...]
    return values * cosine[...] + sign * moved


def pair_masks(length):
    rows = lax.broadcasted_iota(jnp.int32, (length, length), 0)
    columns = lax.broadcasted_iota(jnp.int32, (length, length), 1)
    lanes = lax.broadcasted_iota(jnp.int32, (length, 2 * HEAD), 1)
    return (rows >= columns, lanes < HEAD)


def score(query, keyed, causal):
    return jnp.where(causal, product(query, keyed, ((1,), (1,))), mask_fill)


def soft(scores):
    top = jnp.max(scores, axis=-1, keepdims=True)
    weights = jnp.exp(scores - top)
    total = jnp.sum(weights, axis=-1, keepdims=True)
    return (weights / total, top + jnp.log(total))


def out_columns(weights, inner, piece):
    start, step = (weights.shape[1] - inner, weights.shape[0] // OUTERS)
    rows = step // MEMBERS
    return jnp.concatenate(
        [weights[k * step + piece * rows : k * step + (piece + 1) * rows, start:] for k in range(OUTERS)], axis=0
    )


def attend_kernel(count, *refs):
    tokens, (weights, norm, bias, *tables) = (refs[:count], refs[count : count + 6])
    normed, turned, mixed, logs, *branches = refs[count + 6 :]
    length, inner = (tokens[0].shape[0], bias.shape[1] // 3)
    causal, first = pair_masks(length)
    for block, part in enumerate(tokens):
        rows = slice(block * length, (block + 1) * length)
        normal, _ = normalize(part[...].astype(FULL))
        normed[rows] = (normal * norm[0:1] + norm[1:2]).astype(LOW)
    projected = product(normed[...], weights[:, : 3 * inner], ((1,), (0,))) + bias[...]
    for block in range(count):
        rows = slice(block * length, (block + 1) * length)
        query = rotate(projected[rows, :inner], tables, 1.0).astype(LOW)
        keyed = rotate(projected[rows, inner : 2 * inner], tables, 1.0).astype(LOW)
        valued = projected[rows, 2 * inner :].astype(LOW)
        turned[rows, :inner] = query
        turned[rows, inner : 2 * inner] = keyed
        turned[rows, 2 * inner :] = valued
        for column in range(0, inner, 2 * HEAD):
            at = slice(column, column + 2 * HEAD)
            outs = []
            for head, side in enumerate((first, ~first), column // HEAD):
                query_one = jnp.where(side, query[:, at] * HEAD**-0.5, 0)
                prob, log = soft(score(query_one, keyed[:, at], causal))
                logs[rows, head : head + 1] = log
                outs.append(product(prob.astype(LOW), valued[:, at], ((1,), (0,))))
            mixed[rows, at] = jnp.where(first, outs[0], outs[1]).astype(LOW)
    half = length * count // 2
    for piece in range(MEMBERS):
        share = product(mixed[...], out_columns(weights, inner, piece), ((1,), (0,))).astype(LOW)
        for at, branch in enumerate(branches):
            branch[:, piece * inner : (piece + 1) * inner] = share[at * half : (at + 1) * half]


def attend(blocks, weights, norm, bias, tables):
    length, width = blocks[0].shape
    rows, inner = (length * len(blocks), bias.shape[1] // 3)
    shapes = [jax.ShapeDtypeStruct((rows, n), LOW) for n in (width, 3 * inner, inner)]
    shapes += [jax.ShapeDtypeStruct((rows, 128), FULL)] + [jax.ShapeDtypeStruct((rows // 2, width), LOW)] * 2
    return pl.pallas_call(
        functools.partial(attend_kernel, len(blocks)),
        out_shape=shapes,
        compiler_params=pltpu.CompilerParams(vmem_limit_bytes=28 << 20),
        cost_estimate=pl.CostEstimate(flops=10**9, bytes_accessed=rows * width, transcendentals=0),
        name="attend",
    )(*blocks, weights, norm, bias, *tables)


def attend_back_kernel(count, places, *refs):
    grads, tokens, refs = (refs[:count], refs[count : 2 * count], refs[2 * count :])
    weights, turned, logs, sums_in, norm_in, *tables = refs[:8]
    back, sums, norm_sums, shares, back_mixed, normed_grad, low_grad, sent = refs[9:]
    length, inner = (grads[0].shape[0], turned.shape[1] // 3)
    total = 0.0
    for piece in range(MEMBERS):
        columns = slice(piece * inner, (piece + 1) * inner)
        rows = jnp.concatenate([grad[:, columns] for grad in grads], axis=0)
        total += product(rows, out_columns(weights, inner, piece), ((1,), (1,)))
    back_mixed[...] = total.astype(LOW)
    causal, first = pair_masks(length)
    bias_total = sums_in[...]
    for block in range(count):
        rows = slice(block * length, (block + 1) * length)
        parts = []
        for column in range(0, inner, 2 * HEAD):
            query, keyed, valued = (
                turned[rows, part * inner + column : part * inner + column + 2 * HEAD] for part in range(3)
            )
            grad_pair = back_mixed[rows, column : column + 2 * HEAD]
            back_query, back_key, back_value = ([], 0.0, 0.0)
            for head, side in enumerate((first, ~first), column // HEAD):
                query_one = jnp.where(side, query * HEAD**-0.5, 0)
                grad_one = jnp.where(side, grad_pair, 0)
                prob = jnp.exp(score(query_one, keyed, causal) - logs[rows, head : head + 1])
                back_value += product(prob.astype(LOW), grad_one, ((0,), (0,)))
                grad_prob = product(grad_one, valued, ((1,), (1,)))
                delta = jnp.sum(prob * grad_prob, axis=-1, keepdims=True)
                grad_scores = (prob * (grad_prob - delta)).astype(LOW)
                back_query.append(product(grad_scores, keyed, ((1,), (0,))))
                back_key += product(grad_scores, query_one, ((0,), (0,)))
            back_query = jnp.where(first, back_query[0], back_query[1]) * HEAD**-0.5
            parts.append((back_query, back_key, back_value))
        back_query, back_key, back_value = (jnp.concatenate(side, axis=1) for side in zip(*parts))
        back[rows, :inner] = rotate(back_query, tables, -1.0).astype(LOW)
        back[rows, inner : 2 * inner] = rotate(back_key, tables, -1.0).astype(LOW)
        back[rows, 2 * inner :] = back_value.astype(LOW)
        bias_total += jnp.sum(back[rows].astype(FULL), axis=0, keepdims=True)
    sums[...] = bias_total
    normed_grad[...] = product(back[...], weights[:, : 3 * inner], ((1,), (1,)))
    scale_total, shift_total = (norm_in[0:8], norm_in[8:16])
    leaving = []
    for block in range(count):
        rows = slice(block * length, (block + 1) * length)
        low_grad[rows] = normed_grad[rows].astype(LOW)
        there = pl.ds(pl.multiple_of(places[block] * length, length), length)
        leaving.append(pltpu.make_async_copy(low_grad.at[rows], shares.at[there], sent.at[block]))
        leaving[-1].start()
    for block in range(count):
        rows = slice(block * length, (block + 1) * length)
        grad = normed_grad[rows]
        normal, _ = normalize(tokens[block][...].astype(FULL))
        scale_total += jnp.sum(grad * normal, axis=0, keepdims=True)
        shift_total += jnp.sum(grad, axis=0, keepdims=True)
    norm_sums[0:8] = scale_total
    norm_sums[8:16] = shift_total
    for copy in leaving:
        copy.wait()


def attend_back(places, grads, tokens, weights, turned, logs, sums, norm_sums, shares, tables, micros):
    length, width = grads[0].shape
    count, (rows, columns) = (len(grads), turned.shape)
    made = (jax.ShapeDtypeStruct((rows, columns), LOW), sums, norm_sums, shares)
    operands = (places, *grads, *tokens, weights, turned, logs, sums, norm_sums, *tables, shares)
    vmem, away = (pl.BlockSpec(memory_space=pltpu.VMEM), pl.BlockSpec(memory_space=pltpu.HBM))
    return pl.pallas_call(
        functools.partial(attend_back_kernel, count),
        in_specs=[pl.BlockSpec(memory_space=pltpu.SMEM)] + [vmem] * (len(operands) - 2) + [away],
        out_specs=[vmem] * 3 + [away],
        out_shape=[jax.ShapeDtypeStruct(m.shape, m.dtype) for m in made],
        scratch_shapes=[
            pltpu.VMEM((rows, columns // 3), LOW),
            pltpu.VMEM((rows, width), FULL),
            pltpu.VMEM((rows, width), LOW),
            pltpu.SemaphoreType.DMA((count,)),
        ],
        input_output_aliases={len(operands) - 1: 3},
        compiler_params=pltpu.CompilerParams(vmem_limit_bytes=28 << 20),
        cost_estimate=pl.CostEstimate(flops=micros * 10**9, bytes_accessed=rows * width, transcendentals=0),
        name="attend_back",
    )(*operands)


def residual_kernel(tokens, mine, arrived, twin, norm, residual, normed):
    total = tokens[...].astype(FULL) + mine[...].astype(FULL) + arrived[...].astype(FULL) + twin[...].astype(FULL)
    residual[...] = total
    normal, _ = normalize(total)
    normed[...] = (normal * norm[2:3] + norm[3:4]).astype(LOW)


def norm_back_kernel(given, row, low, values, base, *refs):
    grad = sum(g[...].astype(FULL) for g in refs[:given])
    norm, outs = (refs[given], refs[given + 1 :])
    normal, scaled = normalize(values[...].astype(FULL))
    total = base[...].astype(FULL) + norm_back(grad, normal, scaled, norm[row : row + 1])
    outs[0][...] = total
    if low:
        outs[1][...] = total.astype(LOW)

        @pl.when(pl.program_id(0) == 0)
        def _():
            outs[2][...] = jnp.zeros_like(outs[2])

        outs[2][0:8] += jnp.broadcast_to(jnp.sum(grad * normal, axis=0, keepdims=True), (8, grad.shape[1]))
        outs[2][8:16] += jnp.broadcast_to(jnp.sum(grad, axis=0, keepdims=True), (8, grad.shape[1]))


def by_rows(kernel, rows, operands, norm, shapes, name):
    block = rows // 2
    width = operands[0].shape[1]
    spot = pl.BlockSpec((block, width), lambda i: (i, 0))
    whole = [pl.BlockSpec(norm.shape, lambda i: (0, 0))] if norm is not None else []
    return pl.pallas_call(
        kernel,
        grid=(rows // block,),
        in_specs=[spot] * len(operands) + whole,
        out_specs=[spot if shape[0] == rows else pl.BlockSpec(shape, lambda i: (0, 0)) for shape, _ in shapes],
        out_shape=[jax.ShapeDtypeStruct(shape, kind) for shape, kind in shapes],
        compiler_params=pltpu.CompilerParams(vmem_limit_bytes=16 << 20),
        cost_estimate=pl.CostEstimate(flops=10**8, bytes_accessed=10**6, transcendentals=0),
        name=name,
    )(*operands, *([norm] if whole else []))


def join_kernel(first, second, both):
    rows = first.shape[0]
    both[:rows] = first[...]
    both[rows:] = second[...]


def join_rows(first, second):
    rows, width = first.shape
    return pl.pallas_call(
        join_kernel,
        out_shape=jax.ShapeDtypeStruct((2 * rows, width), first.dtype),
        compiler_params=pltpu.CompilerParams(vmem_limit_bytes=8 << 20),
        cost_estimate=pl.CostEstimate(flops=1, bytes_accessed=1, transcendentals=0),
        name="join_rows",
    )(first, second)


def weight_grad_kernel(sizes, *refs):
    out, at, column = (refs[-1], 0, 0)
    for count in sizes:
        if count:
            lefts, rights = (refs[at : at + count[0]], refs[at + count[0] : at + sum(count)])
            total, rights = (0.0, list(rights))
            for left in lefts:
                right = [rights.pop(0)[...]]
                while sum(r.shape[0] for r in right) < left.shape[0]:
                    right.append(rights.pop(0)[...])
                total += product(left[...], jnp.concatenate(right, axis=0), ((0,), (0,)))
            at += sum(count)
        else:
            total = refs[at][...]
            if total.shape[0] == 8:
                total = jnp.concatenate([total, jnp.zeros((120, total.shape[1]), FULL)], axis=0).T
            at += 1
        out[:, column : column + total.shape[1]] = total.astype(LOW)
        column += total.shape[1]


def weight_grad(terms, block, limit):
    sizes, operands, specs, wide = ([], [], [], 0)
    for term in terms:
        if isinstance(term, tuple):
            lefts, rights = term
            height = lefts[0].shape[1]
            rows = min(block, height)
            columns = rights[0].shape[1]
            sizes.append((len(lefts), len(rights)))
            operands += [*lefts, *rights]
            specs += [pl.BlockSpec((left.shape[0], rows), lambda i: (0, i)) for left in lefts]
            specs += [pl.BlockSpec(right.shape, lambda i: (0, 0)) for right in rights]
        elif term.shape[0] == 8:
            columns = 128
            sizes.append(())
            operands.append(term)
            specs.append(pl.BlockSpec((8, rows), lambda i: (0, i)))
        else:
            columns = term.shape[1]
            sizes.append(())
            operands.append(term)
            specs.append(pl.BlockSpec((rows, columns), lambda i: (i, 0)))
        wide += columns
    return pl.pallas_call(
        functools.partial(weight_grad_kernel, tuple(sizes)),
        grid=(height // rows,),
        in_specs=specs,
        out_specs=pl.BlockSpec((rows, wide), lambda i: (i, 0)),
        out_shape=jax.ShapeDtypeStruct((height, wide), LOW),
        compiler_params=pltpu.CompilerParams(vmem_limit_bytes=limit << 20),
        cost_estimate=pl.CostEstimate(flops=height * wide, bytes_accessed=height * wide, transcendentals=0),
        name="weight_grad",
    )(*operands)


def attn_grad_kernel(count, place, *refs):
    lefts, rights = (refs[:count], refs[count : 2 * count])
    one, two, bias, packed, first, second = refs[2 * count :]
    grad = 0.0
    for left, right in zip(lefts, rights):
        grad += product(left[...], right[...], ((0,), (0,)))
    columns, rows = (grad.shape[1], grad.shape[0] // RING)
    small = jnp.concatenate([one[0:1], one[8:9], two[0:1], two[8:9], bias[0:4]], axis=0)
    small = jnp.concatenate([small, jnp.zeros((120, small.shape[1]), FULL)], axis=0).T
    for z in range(RING):
        spot = lax.rem(z + RING - place[1], RING)
        for half, (out, at) in enumerate(((first, (0, spot)), (second, (spot, 0)))):
            here = slice(z * rows + half * rows // 2, z * rows + (half + 1) * rows // 2)
            out[(*at, slice(None), slice(0, columns))] = grad[here].astype(LOW)
            out[(*at, slice(None), slice(columns, columns + 128))] = small[here].astype(LOW)
            out[(*at, slice(None), slice(columns + 128, None))] = packed[here]


def attn_grads(lefts, rights, norm_one, norm_two, bias, packed):
    width, columns = (lefts[0].shape[1], rights[0].shape[1])
    wide, rows = (columns + 128 + packed.shape[1], width // RING)
    place = jnp.stack([lax.axis_index(axis) for axis in OUTER]).astype(jnp.int32)
    half = rows // RING // 2

    def here(j, place):
        return lax.rem(place[0] + j, RING)

    return pl.pallas_call(
        functools.partial(attn_grad_kernel, len(lefts)),
        grid_spec=pltpu.PrefetchScalarGridSpec(
            num_scalar_prefetch=1,
            grid=(RING,),
            in_specs=[pl.BlockSpec((left.shape[0], rows), lambda j, place: (0, here(j, place))) for left in lefts]
            + [pl.BlockSpec(right.shape, lambda j, place: (0, 0)) for right in rights]
            + [pl.BlockSpec((a.shape[0], rows), lambda j, place: (0, here(j, place))) for a in (norm_one, norm_two, bias)]
            + [pl.BlockSpec((rows, packed.shape[1]), lambda j, place: (here(j, place), 0))],
            out_specs=[
                pl.BlockSpec((1, RING, half, wide), lambda j, place: (j, 0, 0, 0)),
                pl.BlockSpec((RING, 1, half, wide), lambda j, place: (0, j, 0, 0)),
            ],
        ),
        out_shape=[jax.ShapeDtypeStruct((RING, RING, half, wide), LOW)] * 2,
        compiler_params=pltpu.CompilerParams(vmem_limit_bytes=60 << 20),
        cost_estimate=pl.CostEstimate(flops=10**9, bytes_accessed=10**6, transcendentals=0),
        name="attn_grads",
    )(place, *lefts, *rights, norm_one, norm_two, bias, packed)


def out_grad_kernel(count, *refs):
    mixed, grads, packed = (refs[:count], list(refs[count:-1]), refs[-1])
    total = 0.0
    for left in mixed:
        right = []
        while sum(r.shape[0] for r in right) < left.shape[0]:
            right.append(grads.pop(0)[...])
        total += product(left[...], jnp.concatenate(right, axis=0), ((0,), (0,)))
    total = total.astype(LOW)
    step, inner = (packed.shape[0] // OUTERS, packed.shape[1])
    rows = step // MEMBERS
    for outer in range(OUTERS):
        for piece in range(MEMBERS):
            start = outer * step + piece * rows
            packed[start : start + rows] = total[outer * rows : (outer + 1) * rows, piece * inner : (piece + 1) * inner]


def packed_out_grad(mixed, grads):
    width, inner = (grads[0].shape[1], mixed[0].shape[1])
    return pl.pallas_call(
        functools.partial(out_grad_kernel, len(mixed)),
        out_shape=jax.ShapeDtypeStruct((width, inner), LOW),
        compiler_params=pltpu.CompilerParams(vmem_limit_bytes=16 << 20),
        cost_estimate=pl.CostEstimate(flops=width * inner, bytes_accessed=width * inner, transcendentals=0),
        name="out_grad",
    )(*mixed, *grads)


def adamw(weight, grad, first, second, rate, decay):
    first_new = beta_one * first + (1.0 - beta_one) * grad
    second_new = beta_two * second + (1.0 - beta_two) * grad * grad
    corr_one = 1.0 - beta_one**STEP
    corr_two = 1.0 - beta_two**STEP
    update = first_new / corr_one / (jnp.sqrt(second_new / corr_two) + adam_eps)
    return (weight - rate * (update + decay * weight), first_new, second_new)


def adamw_kernel(skip, pieces, weight, first, second, *outs):
    rows, wide = (weight.shape[0], weight.shape[1] // (pieces.shape[0] // 2))
    half = wide // 2
    across = -(-half // 128) * 128
    lanes = lax.broadcasted_iota(jnp.int32, (rows, wide), 1)
    blank = jnp.zeros((rows, wide - across), FULL)

    def turned(member, start, target):
        base = start // 128 * 128
        values = pieces[member, :, base : base + across].astype(FULL)
        move = (target - (start - base)) % across
        return pltpu.roll(values, move, 1) if move else values

    for part in range(3):

        @pl.when(pl.program_id(0) == part)
        def _():
            start = skip + part * half
            for pair in range(pieces.shape[0] // 2):
                left = jnp.concatenate([turned(2 * pair, start, 0), blank], axis=1)
                right = jnp.concatenate([blank, turned(2 * pair + 1, start, across - half)], axis=1)
                grad = jnp.where(lanes < half, left, right)
                at = (slice(None), slice(pair * wide, (pair + 1) * wide))
                made = adamw(weight[at], grad, first[at], second[at], rate_matrix, decay_matrix)
                for out, value in zip(outs, made):
                    out[at] = value


def adamw_mlp(pieces, skip, weight, first, second):
    rows, width = weight.shape
    spot = pl.BlockSpec((rows, width // 3), lambda part: (0, part))
    return pl.pallas_call(
        functools.partial(adamw_kernel, skip),
        grid=(3,),
        in_specs=[pl.BlockSpec(pieces.shape, lambda part: (0, 0, 0))] + [spot] * 3,
        out_specs=[spot] * 3,
        out_shape=[jax.ShapeDtypeStruct(weight.shape, FULL)] * 3,
        compiler_params=pltpu.CompilerParams(vmem_limit_bytes=24 << 20),
        cost_estimate=pl.CostEstimate(flops=10**8, bytes_accessed=7 * 4 * weight.size, transcendentals=0),
        name="adamw",
    )(pieces, weight, first, second)


def shift(values, axis, hop):
    return lax.ppermute(values, axis, [(i, (i + hop) % RING) for i in range(RING)])


def sibling(values):
    return lax.ppermute(values, "core", [(0, 1), (1, 0)])


def add(*values):
    return sum(v.astype(FULL) for v in values)


def hold(values, *others):
    return lax.optimization_barrier((values, others))[0]


def blocks_at(rows, places, length, column):
    width = rows.shape[1] // 2
    return [lax.dynamic_slice(rows, (place * length, column), (length, width)) for place in places]


def onward(values, back=False):
    moves = []
    for chip in range(RING):
        for core, hop in ((0, 1), (1, -1)):
            moves.append((2 * chip + core, 2 * ((chip + (-hop if back else hop)) % RING) + core))
    return lax.ppermute(values, GROUP, moves)


def group_places():
    chip, core = (lax.axis_index(axis) for axis in GROUP)
    one, two, far = ((chip + 3 + 2 * core) % RING, (chip + 1 + 2 * core) % RING, (chip + 2) % RING)
    other = 1 - core
    parts = (
        [2 * chip + core, 2 * chip + other],
        [2 * one + core, 2 * one + other, 2 * two + other, 2 * two + core],
        [2 * far + core, 2 * far + other],
    )
    return [jnp.stack(part).astype(jnp.int32) for part in parts]


def gather_group(values, work):
    rows = values.shape[0]
    own = join_rows(values, sibling(values))
    one = onward(own)
    parts = [[own[:rows], own[rows:]]]
    done = [work(0, parts[0])]
    one = hold(one, done[0][-1])
    far = onward(one[:rows])
    two = sibling(one)
    parts.append([one[:rows], one[rows:], two[:rows], two[rows:]])
    done.append(work(1, parts[1]))
    far = hold(far, done[1][-1])
    parts.append([far, sibling(far)])
    done.append(work(2, parts[2]))
    return (parts, done)


class Scatter:
    def far(self, blocks):
        self.sum = add(blocks[0], sibling(blocks[1])).astype(LOW)
        return self.sum

    def first(self):
        self.arrived = onward(self.sum, back=True)
        return self.arrived

    def near(self, blocks):
        self.both = add(blocks[0], sibling(blocks[1]))
        self.rows = self.both.shape[0] // 2
        return self.both

    def merge(self):
        rows = self.rows
        low = self.both.astype(LOW)
        self.sum = lax.dynamic_update_slice_in_dim(low, add(self.both[:rows], self.arrived).astype(LOW), 0, 0)
        return self.sum

    def second(self):
        self.arrived = onward(self.sum, back=True)
        return self.arrived

    def own(self, whole):
        rows = self.rows
        twin = sibling(add(whole[rows:], self.arrived[rows:]).astype(LOW))
        return (whole, self.arrived, twin)


def gather_outer(values):
    rows, columns = values.shape
    half = rows // 2
    place = {axis: lax.axis_index(axis) for axis in OUTER}

    def ring(block, axis, straight=False):
        before = shift(block, axis, 1)
        after = shift(block, axis, -1)
        if straight:
            return zip((block, before, after, shift(block, axis, 2)), [(place[axis] + j) % RING for j in (0, 3, 1, 2)], (0,) * 4)
        quarter = block.shape[0] // 2
        far = (shift(before[:quarter], axis, 1), shift(after[quarter:], axis, -1))
        spots = [(place[axis] + j) % RING for j in (0, 3, 1, 2, 2)]
        return zip((block, before, after, *far), spots, (0, 0, 0, 0, quarter))

    lines = []
    for axis, block in (("z", values[:half]), ("y", values[half:])):
        line = jnp.zeros((RING, half, columns), values.dtype)
        for piece, spot, start in ring(block, axis, True):
            line = lax.dynamic_update_slice(line, piece[None], (spot, start, 0))
        lines.append(line)
    whole = jnp.zeros((RING, RING, 2, half, columns), values.dtype)
    rings = [list(ring(line, axis)) for line, axis in zip(lines, ("y", "z"))]
    for piece, spot, start in rings[0]:
        whole = lax.dynamic_update_slice(whole, piece[None, :, None], (spot, start, 0, 0, 0))
    for piece, spot, start in rings[1]:
        whole = lax.dynamic_update_slice(whole, piece[:, None, None], (start, spot, 1, 0, 0))
    return whole.reshape(OUTERS * rows, columns)


def far_step(far, axis):
    half = far.shape[0] // 2
    return (shift(far[:half], axis, 1), shift(far[half:], axis, -1))


def near_shares(next_part, last_part, arrived):
    up, down = arrived
    half = up.shape[0]
    after = lax.dynamic_update_slice_in_dim(next_part, add(next_part[:half], up).astype(LOW), 0, 0)
    before = lax.dynamic_update_slice_in_dim(last_part, add(last_part[half:], down).astype(LOW), half, 0)
    return (after, before)


def near_step(shares, axis):
    return (shift(shares[0], axis, 1), shift(shares[1], axis, -1))


def reduce_ring(parts, axis):
    return add(parts[0], *(shift(parts[j], axis, j) for j in (1, 3, 2)))


def ring_order(values, axis, dim):
    place = lax.axis_index(axis)
    return [lax.dynamic_index_in_dim(values, (place + j) % RING, dim, keepdims=False) for j in range(RING)]


def block_moves(back):
    moves = []
    for outer in range(OUTERS):
        for member in range(MEMBERS):
            owner = member * OUTERS + outer
            here = outer * MEMBERS + member
            moves.append((here, owner) if back else (owner, here))
    return moves


def spread_columns(block, parts):
    rows = block.shape[0]
    return block.reshape(rows, parts, MEMBERS, -1).transpose(2, 0, 1, 3).reshape(MEMBERS, rows, -1)


def join_columns(pieces, parts):
    members, rows, width = pieces.shape
    turned = pieces.reshape(members, rows, parts, width // parts).transpose(1, 2, 0, 3)
    return turned.reshape(rows, members * width)


def local(
    tokens,
    cotangent,
    attn_weight,
    mlp_weight,
    small_weight,
    attn_first,
    attn_second,
    mlp_first,
    mlp_second,
    small_first,
    small_second,
):
    length, width = tokens.shape
    own_rows = attn_weight.shape[0]
    slab = own_rows * MEMBERS
    hidden = mlp_weight.shape[1] // 3 // MEMBERS
    inner = width // MEMBERS
    heads = inner // HEAD
    member = lax.axis_index(GROUP)

    rows_all = lax.all_gather(jnp.concatenate([tokens, cotangent], axis=1), GROUP, axis=0, tiled=True)

    attn_low = attn_weight.astype(LOW)
    small_low = jnp.pad(small_weight.astype(LOW).T, ((0, 0), (0, 121)))
    columns = 3 * inner + 128
    sent = jnp.concatenate(
        [
            spread_columns(attn_low[:, : 3 * width], 3),
            jnp.broadcast_to(small_low, (MEMBERS, own_rows, 128)),
            spread_columns(mlp_weight.astype(LOW), 3),
        ],
        axis=2,
    )
    slabs = lax.all_to_all(sent, GROUP, 0, 0, tiled=True).reshape(slab, columns + 3 * hidden)
    out_block = lax.ppermute(attn_low[:, 3 * width :], EVERY, block_moves(False))
    out_block = out_block.reshape(own_rows, MEMBERS, inner).transpose(1, 0, 2).reshape(slab, inner)
    mlp_part = lax.all_gather(slabs[:, columns:], OUTER, axis=0, tiled=True)
    places = group_places()
    tokens_all = [blocks_at(rows_all, part, length, 0) for part in places]
    attn_part = gather_outer(jnp.concatenate([slabs[:, :columns], out_block], axis=1))
    params = attn_part[:, 3 * inner : 3 * inner + 7].T.astype(FULL)
    bias = lax.dynamic_slice_in_dim(params[4:7], member * inner, inner, axis=1).reshape(1, -1)
    weight_wide = mlp_part[:, : 2 * hidden]
    weight_down = mlp_part[:, 2 * hidden :]

    tables = rope_tables(length, length, inner)
    cotangent_all = [jnp.concatenate(blocks_at(rows_all, part, length, width), axis=0) for part in places]

    def forward(blocks):
        return attend(blocks, attn_part, params[:2], bias, tables)

    ring = Scatter()
    kept = {2: forward(tokens_all[2])}
    ring.far(kept[2][4:])
    near_in = hold(tokens_all[1], ring.sum)
    ring.first()
    kept[1] = forward(near_in)
    ring.near(hold(kept[1][4:], ring.arrived))
    own_in, cotangent_all = hold((tokens_all[0], cotangent_all), ring.merge())
    own_in = hold(own_in, cotangent_all)
    ring.second()
    kept[0] = forward(own_in)
    ring.arrived = hold(ring.arrived, kept[0][4:])
    residual, normed_two = by_rows(
        residual_kernel,
        length,
        (tokens, kept[0][4], ring.arrived, sibling(add(kept[0][5], ring.arrived[length:]).astype(LOW))),
        params,
        (((length, width), FULL), ((length, width), LOW)),
        "residual",
    )
    normed_low, turned, mixed_low, logs = ([kept[p][i] for p in range(3)] for i in range(4))

    def feed(part, blocks):
        rows = jnp.concatenate(blocks, axis=0)
        both = product(rows, weight_wide, ((1,), (0,)))
        gate, upward = (both[:, :hidden], both[:, hidden:])
        sigma = jax.nn.sigmoid(gate)
        active = gate * sigma
        hidden_low = (active * upward).astype(LOW)
        back_hidden = product(cotangent_all[part], weight_down, ((1,), (0,)))
        back_gate = (back_hidden * upward * sigma * (1.0 + gate * (1.0 - sigma))).astype(LOW)
        back_wide = jnp.concatenate([back_gate, (back_hidden * active).astype(LOW)], axis=1)
        share = product(back_wide, weight_wide, ((1,), (1,))).astype(LOW)
        return (rows, hidden_low, back_wide, share)

    def halves_of(rows):
        half = rows.shape[0] // 2
        return (rows[:half], rows[half:])

    def out_share(part):
        return product(hidden_low[part], weight_down, ((1,), (1,))).astype(LOW)

    _, done = gather_group(normed_two, feed)
    normed_two, hidden_low, back_wide, shares = (list(made) for made in zip(*done))
    ring = Scatter()
    ring.near(halves_of(shares[1]))
    ring.far(halves_of(shares[2]))
    back_wide = hold(back_wide, ring.sum)
    ring.first()
    mlp_grad = weight_grad([(normed_two, back_wide), (cotangent_all, hidden_low)], 512, 36)
    ring.arrived = hold(ring.arrived, mlp_grad)
    ring.merge()
    hidden_low = hold(hidden_low, ring.sum)
    ring.second()
    out_shares = [out_share(part) for part in range(3)]
    ring.arrived = hold(ring.arrived, out_shares)
    back_residual, back_low, norm_two_grads = by_rows(
        functools.partial(norm_back_kernel, 3, 2, True),
        length,
        (residual, cotangent, *ring.own(shares[0])),
        params,
        (((length, width), FULL), ((length, width), LOW), ((16, width), FULL)),
        "norm_back",
    )
    mlp_grad = lax.psum_scatter(mlp_grad, OUTER, scatter_dimension=0, tiled=True)

    back_sums = [jnp.zeros((8, 3 * inner), FULL), jnp.zeros((16, width), FULL), jnp.zeros((MEMBERS * length, width), LOW)]
    ring = Scatter()
    taken, out_grads = ([], [])

    def backward(part, blocks):
        if part == 1:
            ring.far(hold(halves_of(out_shares[2]), blocks[0]))
            blocks = hold(blocks, ring.sum)
            ring.first()
        elif part == 2:
            blocks = hold(blocks, ring.merge())
            ring.second()
        taken.extend(blocks)
        if part == 2:
            out_grads[:] = [packed_out_grad(mixed_low, taken)]
            blocks = hold(blocks, out_grads)
        made = attend_back(
            places[part], blocks, tokens_all[part], attn_part, turned[part], logs[part], *back_sums, tables, (20, 40, 20)[part]
        )
        back_sums[:] = made[1:]
        if part == 0:
            return (made[0], (made[1], ring.near(halves_of(out_shares[1]))))
        return made[:2]

    _, done = gather_group(back_low, backward)
    back_proj = [made[0] for made in done]

    bias_rows = jnp.pad(
        back_sums[0][0].reshape(3, OUTERS, own_rows), ((0, 5), (0, 0), (0, slab - own_rows))
    ).reshape(8, width)
    back_proj = hold(back_proj, ring.arrived)
    halves = attn_grads(normed_low, back_proj, back_sums[1], norm_two_grads, bias_rows, out_grads[0])
    output = add(residual, *(rows[:length] for rows in ring.own(hold(out_shares[0], halves))))
    parts = [[half[j] for j in range(RING)] for half in halves]
    arrived = [far_step(part[2], axis) for part, axis in zip(parts, OUTER)]
    shares = [near_shares(part[1], part[3], halves) for part, halves in zip(parts, arrived)]
    totals = [
        add(part[0], *near_step(share, axis)).astype(LOW) for part, share, axis in zip(parts, shares, OUTER)
    ]
    back_normed_one = lax.psum_scatter(hold(back_sums[2], shares), GROUP, scatter_dimension=0, tiled=True)
    fill = jnp.zeros((slab, columns), LOW)
    blank = jnp.zeros((slab, -(columns + 3 * hidden) % 128), LOW)
    pieces = jnp.concatenate([fill, mlp_grad, blank], axis=1)
    totals = hold(totals, pieces, output)
    totals = [
        reduce_ring([total[j] for j in range(RING)], axis).astype(LOW) for total, axis in zip(totals, OUTER[::-1])
    ]
    attn_grad = hold(jnp.concatenate(totals, axis=0), back_normed_one)
    (grad_tokens,) = by_rows(
        functools.partial(norm_back_kernel, 1, 0, False),
        length,
        (tokens, back_residual, back_normed_one),
        params,
        (((length, width), FULL),),
        "norm_back",
    )
    out_grad = (
        attn_grad[:, 3 * inner + 128 :]
        .reshape(MEMBERS, own_rows, inner)
        .transpose(1, 0, 2)
        .reshape(own_rows, width)
    )
    bias_grad = attn_grad[:own_rows, 3 * inner : 3 * inner + 128]
    block = lax.ppermute(
        jnp.concatenate([out_grad, bias_grad], axis=1), EVERY, block_moves(True)
    ).astype(FULL)
    pieces = lax.dynamic_update_slice(pieces, attn_grad[:, :columns], (0, 0)).reshape(MEMBERS, own_rows, -1)
    all_pieces = lax.all_to_all(pieces, GROUP, 0, 0, tiled=True)
    pieces = all_pieces[:, :, :columns].astype(FULL)
    attn_grad = jnp.concatenate(
        [join_columns(pieces[:, :, : 3 * inner], 3), block[:, :width]], axis=1
    )
    norm_grads = jnp.sum(pieces[:, :, 3 * inner : 3 * inner + 4], axis=0)
    small_grad = jnp.concatenate([norm_grads, block[:, width + 4 : width + 7]], axis=1).T

    attn_new, attn_first_new, attn_second_new = adamw(
        attn_weight, attn_grad, attn_first, attn_second, rate_matrix, decay_matrix
    )
    mlp_new, mlp_first_new, mlp_second_new = adamw_mlp(all_pieces, columns, mlp_weight, mlp_first, mlp_second)
    small_new, small_first_new, small_second_new = adamw(
        small_weight, small_grad, small_first, small_second, rate_small, 0.0
    )
    return (
        output.astype(LOW),
        grad_tokens,
        attn_new,
        attn_first_new,
        attn_second_new,
        mlp_new,
        mlp_first_new,
        mlp_second_new,
        small_new,
        small_first_new,
        small_second_new,
    )


def solution(mesh):
    grid = Mesh(mesh.devices.reshape(4, 4, 4, 2), EVERY)
    rows, columns = (P(EVERY, None), P(None, EVERY))
    return jax.shard_map(
        local,
        mesh=grid,
        in_specs=(rows,) * 4 + (columns,) + (rows,) * 4 + (columns,) * 2,
        out_specs=(rows,) * 8 + (columns,) * 3,
        check_vma=False,
    )
```
